32 devices in a mesh: seq: 8 (over z, x), head: 4 (over y, core).
Axes of the slice: x: 2, y: 2, z: 4, core: 2. Of those that a mesh axis runs over, the one named last changes fastest.
Arguments:
- tokens: bfloat16 [4096, 4096], P('seq'), may hold values from -6 to 6
- w_xz: bfloat16 [4096, 2, 4096], P('seq', None, 'head'), may hold values from -0.09375 to 0.09375
- w_bc: bfloat16 [4096, 256], P('seq'), may hold values from -0.09375 to 0.09375
- conv_x: float32 [4, 4096], P(None, 'head'), may hold values from -3 to 3
- conv_bc: float32 [4, 256], replicated, may hold values from -3 to 3
- tail_x: bfloat16 [3, 4096], P(None, 'head'), may hold values from -6 to 6
- tail_bc: bfloat16 [3, 256], replicated, may hold values from -6 to 6
- decay_code: int32 [4096, 64], P('seq', 'head'), may hold values from 0 to 49152, as said below
- skip_gain: float32 [64], P('head'), may hold values from 0.5 to 2
- state_in: float32 [64, 64, 128], P('head'), may hold values from -180 to 180
- norm_gain: float32 [4096], P('head'), may hold values from 0.1 to 1.9
- w_out: bfloat16 [4096, 4096], P('head', 'seq'), may hold values from -0.125 to 0.125
Outputs:
- mixed: bfloat16 [4096, 4096], P('seq', 'head')
The draws below stay inside these ranges and needn't reach their ends.
Inputs may be any that keep to these rules, and one draw needn't show every extreme that they name: `decay_code`: the decay factor of a token and head is exp(-code / 65536).
All inputs are finite; a program needn't handle non-finite values.
Results may differ from the reference program's by a relative error of at most 0.0085.
Values may be sent and summed in bfloat16 or wider, within the bound.
No kernel may reach another device: no remote copies, remote signals or barrier semaphores. Data moves between devices by JAX's collectives and lax.ppermute only.
A program may use at most 128 MiB of HBM per device.

```python
import jax
import jax.numpy as jnp
from jax import lax

D = 4096
PARTIAL_SSM_UNIT = 64
P_SIZE = 64
NS = 128
KW = 4
Q = 256
INNER = 4096
SPAN_ENTRIES = 4096


def draw_decay_code(key, part):
    category_entropy_seed, leisurely_entropy_seed, quicker_entropy_seed, spell_entropy_seed, extent_entropy_seed, horizontal_entropy_seed, vertical_entropy_seed = jax.random.split(jax.random.fold_in(key, 11), 7)
    fast = jax.random.randint(category_entropy_seed, (1, PARTIAL_SSM_UNIT), 0, 5) < 2
    slow = jax.random.randint(leisurely_entropy_seed, (SPAN_ENTRIES, PARTIAL_SSM_UNIT), 0, 4)
    quick = jax.random.randint(quicker_entropy_seed, (SPAN_ENTRIES, PARTIAL_SSM_UNIT), 3 * SPAN_ENTRIES // 10, 6 * SPAN_ENTRIES // 10)
    matched_indicator = jax.random.randint(spell_entropy_seed, (SPAN_ENTRIES, PARTIAL_SSM_UNIT), 0, 2048) == 0
    spell_duration = jax.random.randint(extent_entropy_seed, (SPAN_ENTRIES, PARTIAL_SSM_UNIT), 4 * SPAN_ENTRIES, 11 * SPAN_ENTRIES)
    starting_level = jnp.where(fast, quick, slow)
    symbol_entries = jnp.where(matched_indicator, starting_level + spell_duration, starting_level)
    top_row = jax.random.randint(horizontal_entropy_seed, (), 0, SPAN_ENTRIES)
    top_col = jax.random.randint(vertical_entropy_seed, (), 0, PARTIAL_SSM_UNIT)
    places = (jnp.arange(SPAN_ENTRIES)[:, None] == top_row) & (jnp.arange(PARTIAL_SSM_UNIT)[None, :] == top_col)
    return jnp.where(places, 12 * SPAN_ENTRIES, symbol_entries).astype(jnp.int32)


def with_spikes(drawn, stream_key, source, target, blocks, factor):
    owner, partner = [(jnp.arange(drawn.shape[dim]) // (drawn.shape[dim] // blocks)).reshape([-1 if axis == dim else 1 for axis in range(drawn.ndim)]) for dim in (source, target)]
    chosen = jax.random.permutation(stream_key, blocks)[partner]
    strong = (owner == chosen) | (owner == (partner + blocks // 2) % blocks)
    return jnp.where(strong, factor * drawn, drawn)


def steps_of(own_key, extent, shards, low, largest):
    def one(axis_at, shards_of):
        draws = jax.random.uniform(jax.random.fold_in(jax.random.fold_in(own_key, 6), axis_at), (shards_of,), jnp.float32, low / len(shards), largest / len(shards))
        return jnp.repeat(jnp.exp(draws), extent[axis_at] // shards_of).reshape((-1,) + (1,) * (len(extent) - axis_at - 1))

    level = one(*shards[0])
    for cut in shards[1:]:
        level = level * one(*cut)
    return level


def noise(key, shape, scale, limit, shards=(), held_as=jnp.bfloat16):
    gain = steps_of(key, shape, shards, -0.22, 0.18) if shards else 1.0
    values = jax.random.normal(key, shape, jnp.float32) * scale * gain
    return jnp.minimum(jnp.maximum(values, -limit), limit).astype(held_as)


def bell_draw_with(key, extent, scale, bound, pieces, heavy, kind=jnp.bfloat16):
    values = scale * jax.random.normal(key, extent, jnp.float32)
    if pieces:
        values = values * steps_of(key, extent, pieces, -0.22, 0.18)
    return jnp.clip(with_spikes(values, jax.random.fold_in(key, 3), *heavy), -bound, bound).astype(kind)


def setup_inputs(seed: int = 0) -> dict:
    key_list = jax.random.split(jax.random.key(seed), 13)
    return {
        "tokens": noise(key_list[0], (SPAN_ENTRIES, D), 1.0, 6.0, ((0, 8),)),
        "w_xz": noise(key_list[1], (D, 2, INNER), D ** -0.5, 0.09375, ((0, 8), (2, 4))),
        "w_bc": noise(key_list[2], (D, 2 * NS), D ** -0.5, 0.09375, ((0, 8),)),
        "conv_x": noise(key_list[3], (KW, INNER), KW ** -0.5, 3.0, ((1, 4),), jnp.float32),
        "conv_bc": noise(key_list[4], (KW, 2 * NS), KW ** -0.5, 3.0, (), jnp.float32),
        "tail_x": noise(key_list[5], (KW - 1, INNER), 1.0, 6.0, ((1, 4),)),
        "tail_bc": noise(key_list[6], (KW - 1, 2 * NS), 1.0, 6.0),
        "decay_code": draw_decay_code(jax.random.fold_in(key_list[12], 71), 0),
        "skip_gain": jnp.clip(0.5 + 1.5 * jax.random.uniform(key_list[8], (PARTIAL_SSM_UNIT,), jnp.float32) ** steps_of(key_list[8], (PARTIAL_SSM_UNIT,), ((0, 4),), -0.2, 0.2), 0.5, 2.0),
        "state_in": noise(key_list[9], (PARTIAL_SSM_UNIT, P_SIZE, NS), 30.0, 180.0, ((0, 4),), jnp.float32),
        "norm_gain": jnp.clip(1.0 + 0.18 * jax.random.normal(key_list[10], (INNER,), jnp.float32), 0.1, 1.9),
        "w_out": bell_draw_with(key_list[11], (INNER, D), INNER ** -0.5, 0.125, ((0, 4), (1, 8)), (0, 1, 8, 2.0)),
    }


def depthwise(pre, tail, kernel):
    whole = jnp.concatenate([tail, pre], axis=0).astype(jnp.float32)
    length = pre.shape[0]
    total = jnp.zeros((length, pre.shape[1]), jnp.float32)
    for offset in range(kernel.shape[0]):
        total = total + kernel[offset] * whole[offset:offset + length]
    return jax.nn.silu(total).astype(jnp.bfloat16)

def block_step(state, inputs):
    xval, bval, cval, logdec = inputs
    cum = jnp.cumsum(logdec, axis=0)
    span = cum.shape[0]
    places = jnp.arange(span)
    lower = places[:, None] >= places[None, :]
    cumt = cum.T
    diff = cumt[:, :, None] - cumt[:, None, :]
    decay = jnp.where(lower[None], jnp.exp(jnp.where(lower[None], diff, 0.0)), 0.0)
    scores = jnp.dot(cval, bval.T, preferred_element_type=jnp.float32)
    weights = (decay * scores[None]).astype(jnp.bfloat16)
    inner = jnp.einsum('hts,shp->thp', weights.astype(jnp.float32), xval.astype(jnp.float32), precision=lax.Precision.HIGHEST)
    carried = jnp.einsum('tn,hpn->thp', cval.astype(jnp.float32), state, precision=lax.Precision.HIGHEST)
    carried = carried * jnp.exp(cum)[:, :, None]
    tail_decay = jnp.exp(cum[-1][None, :] - cum)
    decayed_b = (tail_decay.T[:, :, None] * bval.astype(jnp.float32)[None]).astype(jnp.bfloat16)
    added = jnp.einsum('hsn,shp->hpn', decayed_b.astype(jnp.float32), xval.astype(jnp.float32), precision=lax.Precision.HIGHEST)
    new_state = jnp.exp(cum[-1])[:, None, None] * state + added
    return (new_state, inner + carried)

def reference(tokens, w_xz, w_bc, conv_x, conv_bc, tail_x, tail_bc, decay_code, skip_gain, state_in, norm_gain, w_out):
    length = tokens.shape[0]
    heads, head_dim, nstate = state_in.shape
    inner = heads * head_dim
    xz = jnp.dot(tokens, w_xz.reshape(tokens.shape[1], 2 * inner), preferred_element_type=jnp.float32)
    x_pre = xz[:, :inner].astype(jnp.bfloat16)
    z_val = xz[:, inner:].astype(jnp.bfloat16)
    bc_pre = jnp.dot(tokens, w_bc, preferred_element_type=jnp.float32).astype(jnp.bfloat16)
    x_conv = depthwise(x_pre, tail_x, conv_x)
    bc_conv = depthwise(bc_pre, tail_bc, conv_bc)
    b_val = bc_conv[:, :nstate]
    c_val = bc_conv[:, nstate:]
    logdec = -decay_code.astype(jnp.float32) / (16.0 * SPAN_ENTRIES)
    blocks = length // Q
    inputs = (x_conv.reshape(blocks, Q, heads, head_dim), b_val.reshape(blocks, Q, nstate), c_val.reshape(blocks, Q, nstate), logdec.reshape(blocks, Q, heads))
    final_state, parts = lax.scan(block_step, state_in, inputs)
    parts = parts.reshape(length, inner)
    y_val = parts / nstate + jnp.repeat(skip_gain, head_dim)[None, :] * x_conv.astype(jnp.float32)
    gated = y_val * jax.nn.silu(z_val.astype(jnp.float32))
    meansq = lax.optimization_barrier(jnp.mean(gated * gated, axis=1, keepdims=True))
    normed = (gated * lax.rsqrt(meansq + 1e-05) * norm_gain[None, :]).astype(jnp.bfloat16)
    return jnp.dot(normed, w_out, preferred_element_type=jnp.float32).astype(jnp.bfloat16)
```

```python
import functools

import jax
import jax.numpy as jnp
from jax import lax
from jax.experimental import pallas as pl
from jax.experimental.pallas import tpu as pltpu
from jax.sharding import PartitionSpec as P

Q = 256
HALO = 16
PAIR = 2
F32 = jnp.float32
BF16 = jnp.bfloat16
VMEM_LIMIT = 48 * 1024 * 1024


def swapped(value, axis, bit):
    size = lax.axis_size(axis)
    return lax.ppermute(value, axis, [(i, i ^ bit) for i in range(size)])


def shifted(value, axis, by):
    size = lax.axis_size(axis)
    return lax.ppermute(value, axis, [(i, i + by) for i in range(size - by)])


def cut(value, index, size, axis):
    return lax.dynamic_slice_in_dim(value, index * size, size, axis)


def spread(own, other, seq_count):
    pieces = {0: own, PAIR: swapped(other, "seq", PAIR)}
    bits = [1 << b for b in range(seq_count.bit_length() - 1)]
    for bit in [b for b in bits if b > PAIR] + [b for b in bits if b < PAIR]:
        for mask in list(pieces):
            pieces[mask | bit] = swapped(pieces[mask], "seq", bit)
    return pieces


def dot(a, b):
    return jnp.dot(a, b, preferred_element_type=F32)


def front_kernel(first_ref, x_ref, bc_ref, tx_ref, tbc_ref, kx_ref, kbc_ref, dec_ref, xc_ref, bcc_ref, f_ref):
    is_first = first_ref[pl.program_id(0)] == 1
    rows = xc_ref.shape[1]

    def conv(pre_ref, tail_ref, k_ref):
        pre = pre_ref[0].astype(F32)
        halo = jnp.where(is_first, tail_ref[...].astype(F32), pre[:HALO])
        whole = jnp.concatenate([halo, pre[HALO:]], axis=0)
        taps = k_ref.shape[0]
        total = jnp.zeros((rows, pre.shape[1]), F32)
        for k in range(taps):
            start = HALO - (taps - 1) + k
            total = total + k_ref[k : k + 1, :] * whole[start : start + rows]
        return (total * jax.nn.sigmoid(total)).astype(BF16)

    x_val = conv(x_ref, tx_ref, kx_ref)
    bc_val = conv(bc_ref, tbc_ref, kbc_ref)
    xc_ref[0] = x_val
    bcc_ref[0] = bc_val
    decayed = (x_val.astype(F32) * dec_ref[0]).astype(BF16)
    nstate = bc_val.shape[1] // 2
    for start in range(0, rows, Q):
        f_ref[0, start // Q] = lax.dot_general(
            bc_val[start : start + Q, :nstate],
            decayed[start : start + Q],
            (((0,), (0,)), ((), ())),
            preferred_element_type=F32,
        )


def intra_kernel(heads, x_ref, bc_ref, cum_ref, cumt_ref, y_ref):
    nstate = bc_ref.shape[2] // 2
    span = x_ref.shape[1]
    head_dim = x_ref.shape[2] // heads
    b_val = bc_ref[0, :, :nstate]
    c_val = bc_ref[0, :, nstate:]
    scores = lax.dot_general(c_val, b_val, (((1,), (1,)), ((), ())), preferred_element_type=F32)
    lower = lax.broadcasted_iota(jnp.int32, (span, span), 0) >= lax.broadcasted_iota(jnp.int32, (span, span), 1)
    scores = jnp.where(lower, scores, 0.0)
    pair = 128 // head_dim
    for start in range(0, heads, pair):
        outs = []
        for h in range(start, start + pair):
            diff = cum_ref[0, :, h : h + 1] - cumt_ref[0, 0, h : h + 1, :]
            weights = (jnp.exp(jnp.where(lower, diff, 0.0)) * scores).astype(BF16)
            outs.append(dot(weights, x_ref[0, :, h * head_dim : (h + 1) * head_dim]))
        y_ref[0, :, start * head_dim : (start + pair) * head_dim] = jnp.concatenate(outs, axis=1)


def gate_kernel(y_ref, x_ref, bc_ref, st_ref, e_ref, skip_ref, z_ref, gain_ref, g_ref, ss_ref):
    nstate = st_ref.shape[2]
    c_val = bc_ref[0, :, nstate:]
    state = st_ref[0, 0]
    high = state.astype(BF16)
    low = (state - high.astype(F32)).astype(BF16)
    carried = dot(c_val, high) + dot(c_val, low)
    y_val = (y_ref[0] + e_ref[0] * carried) / nstate + skip_ref[...] * x_ref[0].astype(F32)
    z_val = z_ref[0].astype(F32)
    gated = y_val * (z_val * jax.nn.sigmoid(z_val))
    g_ref[0] = (gated * gain_ref[...]).astype(BF16)
    total = jnp.sum(gated * gated, axis=1, keepdims=True)
    ss_ref[0] = jnp.broadcast_to(total, ss_ref.shape[1:])


def params(grid):
    return pltpu.CompilerParams(dimension_semantics=("arbitrary",) * grid, vmem_limit_bytes=VMEM_LIMIT)


def whole_block(shape):
    return pl.BlockSpec(shape, lambda *_: (0,) * len(shape))


def front(first, x_pre, bc_pre, tail_x, tail_bc, conv_x, conv_bc, decay):
    _, ext, chans = x_pre.shape
    rows = ext - HALO
    bcw = bc_pre.shape[2]

    def ranged(n, w):
        return pl.BlockSpec((1, n, w), lambda r: (r, 0, 0))

    return pl.pallas_call(
        front_kernel,
        grid=(2,),
        in_specs=[
            pl.BlockSpec(memory_space=pltpu.SMEM),
            ranged(ext, chans),
            ranged(ext, bcw),
            whole_block(tail_x.shape),
            whole_block(tail_bc.shape),
            whole_block(conv_x.shape),
            whole_block(conv_bc.shape),
            ranged(rows, chans),
        ],
        out_specs=[
            ranged(rows, chans),
            ranged(rows, bcw),
            pl.BlockSpec((1, rows // Q, bcw // 2, chans), lambda r: (r, 0, 0, 0)),
        ],
        out_shape=[
            jax.ShapeDtypeStruct((2, rows, chans), BF16),
            jax.ShapeDtypeStruct((2, rows, bcw), BF16),
            jax.ShapeDtypeStruct((2, rows // Q, bcw // 2, chans), F32),
        ],
        compiler_params=params(1),
        name="front",
    )(first, x_pre, bc_pre, tail_x, tail_bc, conv_x, conv_bc, decay)


def intra(x_conv, bc_conv, cum, cumt, heads):
    _, rows, chans = x_conv.shape
    bcw = bc_conv.shape[2]
    blocks = rows // Q

    def tile(w):
        return pl.BlockSpec((1, Q, w), lambda r, i: (r, i, 0))

    work = 2 * rows * Q
    return pl.pallas_call(
        functools.partial(intra_kernel, heads),
        grid=(2, blocks),
        in_specs=[tile(chans), tile(bcw), tile(heads), pl.BlockSpec((1, 1, heads, Q), lambda r, i: (r, i, 0, 0))],
        out_specs=tile(chans),
        out_shape=jax.ShapeDtypeStruct((2, rows, chans), F32),
        compiler_params=params(2),
        cost_estimate=pl.CostEstimate(
            flops=2 * work * (chans + bcw // 2), bytes_accessed=12 * rows * chans, transcendentals=work * heads
        ),
        name="intra",
    )(x_conv, bc_conv, cum, cumt)


def gate(y_in, x_conv, bc_conv, state, grown, skip, z_val, gain):
    _, rows, chans = x_conv.shape
    bcw = bc_conv.shape[2]

    def tile(w):
        return pl.BlockSpec((1, Q, w), lambda r, i: (r, i, 0))

    return pl.pallas_call(
        gate_kernel,
        grid=(2, rows // Q),
        in_specs=[
            tile(chans),
            tile(chans),
            tile(bcw),
            pl.BlockSpec((1, 1, bcw // 2, chans), lambda r, i: (r, i, 0, 0)),
            tile(chans),
            whole_block((1, chans)),
            tile(chans),
            whole_block((1, chans)),
        ],
        out_specs=[tile(chans), tile(128)],
        out_shape=[
            jax.ShapeDtypeStruct((2, rows, chans), BF16),
            jax.ShapeDtypeStruct((2, rows, 128), F32),
        ],
        compiler_params=params(2),
        name="gate",
    )(y_in, x_conv, bc_conv, state, grown, skip, z_val, gain)


def local(
    tokens,
    w_xz,
    w_bc,
    conv_x,
    conv_bc,
    tail_x,
    tail_bc,
    decay_code,
    skip_gain,
    state_in,
    norm_gain,
    w_out,
):
    rows = tokens.shape[0]
    all_heads, head_dim, nstate = state_in.shape
    seq_count = lax.axis_size("seq")
    head_count = lax.axis_size("head")
    inner = all_heads * head_dim * head_count
    me = lax.axis_index("seq")
    mine = lax.axis_index("head")
    half = (me // PAIR) % 2
    heads = all_heads // 2
    chans = heads * head_dim
    depth = w_xz.shape[0]

    before = shifted(tokens[rows - HALO :], "seq", 1)
    ext_own = jnp.concatenate([before, tokens], axis=0)
    share = tokens.shape[1] // head_count
    ext_other = lax.all_gather(
        swapped(cut(ext_own, mine, share, 1), "seq", PAIR), "head", axis=1, tiled=True
    )

    def halves(which):
        part = w_xz[:, which, :]
        return cut(part, half, chans, 1), cut(part, 1 - half, chans, 1)

    x_pieces = spread(*halves(0), seq_count)
    z_pieces = spread(*halves(1), seq_count)
    out_pieces = spread(cut(w_out, half, chans, 0), cut(w_out, 1 - half, chans, 0), seq_count)
    part = depth // head_count
    w_bc_all = lax.all_gather(cut(w_bc, mine, part, 0), ("seq", "head"), axis=0, tiled=True)

    logdec = -decay_code.astype(F32) / (16.0 * rows * seq_count)
    ld_own = cut(logdec, half, heads, 1)
    ld = jnp.stack([ld_own, swapped(cut(logdec, 1 - half, heads, 1), "seq", PAIR)])
    blocks = rows // Q
    cum = jnp.cumsum(ld.reshape(2, blocks, Q, heads), axis=2)
    cumt = cum.transpose(0, 1, 3, 2)
    ends = cum[:, :, -1:, :]
    remaining = jnp.repeat(jnp.exp(ends - cum).reshape(2, rows, heads), head_dim, axis=2)
    block_decay = jnp.repeat(jnp.exp(ends), head_dim, axis=3)
    cum = cum.reshape(2, rows, heads)
    grown = jnp.repeat(jnp.exp(cum), head_dim, axis=2)
    totals = lax.all_gather(jnp.sum(logdec, axis=0), "seq", axis=0)
    totals = cut(totals, half, heads, 1)
    places = jnp.arange(seq_count)

    def decay_between(low, high):
        chosen = jnp.where((places >= low) & (places < high), 1.0, 0.0)[:, None]
        return jnp.repeat(jnp.exp(jnp.sum(chosen * totals, axis=0)), head_dim)[None, :]

    def project(ext, pieces):
        total = None
        for mask, piece in pieces.items():
            term = dot(cut(ext, me ^ mask, depth, 1), piece)
            total = term if total is None else total + term
        return total.astype(BF16)

    x_pre = jnp.stack([project(ext_own, x_pieces), project(ext_other, x_pieces)])
    bc_pre = jnp.stack([dot(ext_own, w_bc_all).astype(BF16), dot(ext_other, w_bc_all).astype(BF16)])
    z_val = jnp.stack([project(tokens, z_pieces), project(ext_other[HALO:], z_pieces)])

    ranges = [me, me ^ PAIR]
    first = jnp.stack([(r == 0).astype(jnp.int32) for r in ranges])

    def padded(tail):
        return jnp.pad(tail, ((HALO - tail.shape[0], 0), (0, 0)))

    x_conv, bc_conv, added = front(
        first,
        x_pre,
        bc_pre,
        padded(cut(tail_x, half, chans, 1)),
        padded(tail_bc),
        cut(conv_x, half, chans, 1),
        conv_bc,
        remaining,
    )

    inside = [jnp.zeros_like(added[:, 0])]
    for b in range(blocks):
        inside.append(block_decay[:, b] * inside[-1] + added[:, b])
    ending = inside.pop()

    group = 4
    across = swapped(ending.astype(BF16), "seq", 1).astype(F32)
    ended = {0: ending[0], PAIR: ending[1], 1: across[0], PAIR | 1: across[1]}
    base = (me // group) * group
    groups = seq_count // group
    total = 0.0
    for mask, value in ended.items():
        total = total + decay_between((me ^ mask) + 1, base + group) * value
    carry = shifted(total.astype(BF16), "seq", group).astype(F32)
    covered = 1
    while covered < groups - 1:
        more = shifted(carry.astype(BF16), "seq", group * covered).astype(F32)
        carry = carry + decay_between(base - group * covered, base) * more
        covered *= 2
    begin = cut(state_in, half, heads, 0).transpose(2, 0, 1).reshape(nstate, chans)
    incoming = []
    for place in ranges:
        value = decay_between(0, place) * begin + decay_between(base, place) * carry
        for mask, ended_value in ended.items():
            scale = jnp.where((me ^ mask) < place, decay_between((me ^ mask) + 1, place), 0.0)
            value = value + scale * ended_value
        incoming.append(value)
    opening = jnp.stack(incoming)
    states = []
    for b in range(blocks):
        states.append(opening + inside[b])
        opening = block_decay[:, b] * opening

    y_in = intra(x_conv, bc_conv, cum, cumt, heads)
    gated, squares = gate(
        y_in,
        x_conv,
        bc_conv,
        jnp.stack(states, axis=1),
        grown,
        jnp.repeat(cut(skip_gain, half, heads, 0), head_dim)[None, :],
        z_val,
        cut(norm_gain, half, chans, 0)[None, :],
    )

    squares = squares[0, :, 0] + swapped(squares[1, :, 0], "seq", PAIR)
    bit = 1
    while bit < head_count:
        squares = squares + swapped(squares, "head", bit)
        bit *= 2
    scale = lax.rsqrt(squares / inner + 1e-05)[:, None]

    per = seq_count // head_count
    stacked = jnp.stack([out_pieces[mask] for mask in range(seq_count)])

    def columns(relative):
        base_piece = (mine ^ relative) * per
        return [lax.dynamic_index_in_dim(stacked, me ^ (base_piece + j), 0, keepdims=False) for j in range(per)]

    near = jnp.concatenate([c for r in range(0, head_count, 2) for c in columns(r)], axis=1)
    far = jnp.concatenate([c for r in range(1, head_count, 2) for c in columns(r)], axis=1)
    flat = gated.reshape(2 * rows, chans)
    received = swapped(dot(flat, far).astype(BF16), "head", 1)
    sums = dot(flat, near) + received.astype(F32)
    sums = sums.reshape(2, rows, head_count // 2, -1)

    def fold_head(value):
        count = value.shape[2]
        while count > 1:
            count //= 2
            got = swapped(value[:, :, count:].astype(BF16), "head", 2 * count)
            value = value[:, :, :count] + got.astype(F32)
        return value

    def fold_pair(value):
        return value[:1] + swapped(value[1:].astype(BF16), "seq", PAIR).astype(F32)

    width = sums.shape[3] // 2
    left = fold_pair(fold_head(sums[..., :width]))
    right = fold_head(fold_pair(sums[..., width:]))
    result = jnp.concatenate([left, right], axis=3).reshape(rows, 2 * width)
    return (result * scale).astype(BF16)


def solution(mesh):
    return jax.shard_map(
        local,
        mesh=mesh,
        in_specs=(
            P("seq", None),
            P("seq", None, "head"),
            P("seq", None),
            P(None, "head"),
            P(),
            P(None, "head"),
            P(),
            P("seq", "head"),
            P("head"),
            P("head", None, None),
            P("head"),
            P("head", "seq"),
        ),
        out_specs=P("seq", "head"),
        check_vma=False,
    )
```

```python
import functools

import jax
import jax.numpy as jnp
from jax import lax
from jax.experimental import pallas as pl
from jax.experimental.pallas import tpu as pltpu
from jax.sharding import PartitionSpec as P

Q = 256
HALO = 16
PAIR = 2
F32 = jnp.float32
BF16 = jnp.bfloat16
VMEM_LIMIT = 48 * 1024 * 1024


def swapped(value, axis, bit):
    size = lax.axis_size(axis)
    return lax.ppermute(value, axis, [(i, i ^ bit) for i in range(size)])


def shifted(value, axis, by):
    size = lax.axis_size(axis)
    return lax.ppermute(value, axis, [(i, i + by) for i in range(size - by)])


def cut(value, index, size, axis):
    return lax.dynamic_slice_in_dim(value, index * size, size, axis)


def after(value, *others):
    return lax.optimization_barrier((value, *others))[0]


def spread(own, other, seq_count, earlier=None):
    bits = [1 << b for b in range(seq_count.bit_length() - 1)]
    bits = [b for b in bits if b > PAIR] + [b for b in bits if b < PAIR]
    if earlier is not None:
        other = after(other, earlier[PAIR])
    pieces = {0: own, PAIR: swapped(other, "seq", PAIR)}
    for bit in bits:
        for mask in list(pieces):
            value = pieces[mask]
            if mask == 0 and earlier is not None:
                value = after(value, earlier[bit] if bit > PAIR else earlier[PAIR | bit])
            pieces[mask | bit] = swapped(value, "seq", bit)
    return pieces


def natural(value, axis_name, bit, axis):
    other = swapped(value, axis_name, bit)
    low = (lax.axis_index(axis_name) & bit) == 0
    return jnp.where(
        low, jnp.concatenate([value, other], axis=axis), jnp.concatenate([other, value], axis=axis)
    )


def by_xor(values, index):
    bit = 1
    while bit < len(values):
        flip = (index & bit) != 0
        values = [jnp.where(flip, values[j ^ bit], values[j]) for j in range(len(values))]
        bit *= 2
    return values


def dot(a, b):
    return jnp.dot(a, b, preferred_element_type=F32)


def front_kernel(
    first_ref, xo_ref, xp_ref, bo_ref, bp_ref, tx_ref, tbc_ref, kx_ref, kbc_ref, dec_ref, xc_ref, bcc_ref, f_ref
):
    rows = xc_ref.shape[1]
    for r in range(2):
        is_first = first_ref[r] == 1

        def conv(own_ref, other_ref, tail_ref, k_ref):
            halo = own_ref[r * HALO : (r + 1) * HALO].astype(F32)
            halo = jnp.where(is_first, tail_ref[...].astype(F32), halo)
            body = (own_ref[2 * HALO :] if r == 0 else other_ref[...]).astype(F32)
            whole = jnp.concatenate([halo, body], axis=0)
            taps = k_ref.shape[0]
            total = jnp.zeros(body.shape, F32)
            for k in range(taps):
                start = HALO - (taps - 1) + k
                total = total + k_ref[k : k + 1, :] * whole[start : start + rows]
            return (total * jax.nn.sigmoid(total)).astype(BF16)

        x_val = conv(xo_ref, xp_ref, tx_ref, kx_ref)
        bc_val = conv(bo_ref, bp_ref, tbc_ref, kbc_ref)
        xc_ref[r] = x_val
        bcc_ref[r] = bc_val
        decayed = (x_val.astype(F32) * dec_ref[r]).astype(BF16)
        nstate = bc_val.shape[1] // 2
        for start in range(0, rows, Q):
            f_ref[r, start // Q] = lax.dot_general(
                bc_val[start : start + Q, :nstate],
                decayed[start : start + Q],
                (((0,), (0,)), ((), ())),
                preferred_element_type=F32,
            )


def intra_kernel(heads, x_ref, bc_ref, cum_ref, cumt_ref, y_ref):
    nstate = bc_ref.shape[2] // 2
    span = x_ref.shape[1]
    head_dim = x_ref.shape[2] // heads
    b_val = bc_ref[0, :, :nstate]
    c_val = bc_ref[0, :, nstate:]
    scores = lax.dot_general(c_val, b_val, (((1,), (1,)), ((), ())), preferred_element_type=F32)
    lower = lax.broadcasted_iota(jnp.int32, (span, span), 0) >= lax.broadcasted_iota(jnp.int32, (span, span), 1)
    scores = jnp.where(lower, scores, 0.0)
    pair = 128 // head_dim
    for start in range(0, heads, pair):
        outs = []
        for h in range(start, start + pair):
            diff = cum_ref[0, :, h : h + 1] - cumt_ref[0, 0, h : h + 1, :]
            weights = (jnp.exp(jnp.where(lower, diff, 0.0)) * scores).astype(BF16)
            outs.append(dot(weights, x_ref[0, :, h * head_dim : (h + 1) * head_dim]))
        y_ref[0, :, start * head_dim : (start + pair) * head_dim] = jnp.concatenate(outs, axis=1)


def gate_kernel(y_ref, x_ref, bc_ref, st_ref, e_ref, skip_ref, z_ref, gain_ref, g_ref, ss_ref):
    nstate = st_ref.shape[2]
    c_val = bc_ref[0, :, nstate:]
    state = st_ref[0, 0]
    high = state.astype(BF16)
    low = (state - high.astype(F32)).astype(BF16)
    carried = dot(c_val, high) + dot(c_val, low)
    y_val = (y_ref[0] + e_ref[0] * carried) / nstate + skip_ref[...] * x_ref[0].astype(F32)
    z_val = z_ref[0].astype(F32)
    gated = y_val * (z_val * jax.nn.sigmoid(z_val))
    g_ref[0] = (gated * gain_ref[...]).astype(BF16)
    total = jnp.sum(gated * gated, axis=1, keepdims=True)
    ss_ref[0] = jnp.broadcast_to(total, ss_ref.shape[1:])


def params(grid):
    return pltpu.CompilerParams(dimension_semantics=("arbitrary",) * grid, vmem_limit_bytes=VMEM_LIMIT)


def whole_block(shape):
    return pl.BlockSpec(shape, lambda *_: (0,) * len(shape))


def front(first, x_own, x_other, bc_own, bc_other, tail_x, tail_bc, conv_x, conv_bc, decay):
    rows, chans = x_other.shape
    bcw = bc_other.shape[1]
    return pl.pallas_call(
        front_kernel,
        in_specs=[pl.BlockSpec(memory_space=pltpu.SMEM)] + [pl.BlockSpec(memory_space=pltpu.VMEM)] * 9,
        out_specs=[pl.BlockSpec(memory_space=pltpu.VMEM)] * 3,
        out_shape=[
            jax.ShapeDtypeStruct((2, rows, chans), BF16),
            jax.ShapeDtypeStruct((2, rows, bcw), BF16),
            jax.ShapeDtypeStruct((2, rows // Q, bcw // 2, chans), F32),
        ],
        compiler_params=pltpu.CompilerParams(vmem_limit_bytes=VMEM_LIMIT),
        name="front",
    )(first, x_own, x_other, bc_own, bc_other, tail_x, tail_bc, conv_x, conv_bc, decay)


def intra(x_conv, bc_conv, cum, cumt, heads):
    _, rows, chans = x_conv.shape
    bcw = bc_conv.shape[2]
    blocks = rows // Q

    def tile(w):
        return pl.BlockSpec((1, Q, w), lambda r, i: (r, i, 0))

    work = 2 * rows * Q
    return pl.pallas_call(
        functools.partial(intra_kernel, heads),
        grid=(2, blocks),
        in_specs=[tile(chans), tile(bcw), tile(heads), pl.BlockSpec((1, 1, heads, Q), lambda r, i: (r, i, 0, 0))],
        out_specs=tile(chans),
        out_shape=jax.ShapeDtypeStruct((2, rows, chans), F32),
        compiler_params=params(2),
        cost_estimate=pl.CostEstimate(
            flops=2 * work * (chans + bcw // 2), bytes_accessed=12 * rows * chans, transcendentals=work * heads
        ),
        name="intra",
    )(x_conv, bc_conv, cum, cumt)


def gate(y_in, x_conv, bc_conv, state, grown, skip, z_val, gain):
    _, rows, chans = x_conv.shape
    bcw = bc_conv.shape[2]

    def tile(w):
        return pl.BlockSpec((1, Q, w), lambda r, i: (r, i, 0))

    return pl.pallas_call(
        gate_kernel,
        grid=(2, rows // Q),
        in_specs=[
            tile(chans),
            tile(chans),
            tile(bcw),
            pl.BlockSpec((1, 1, bcw // 2, chans), lambda r, i: (r, i, 0, 0)),
            tile(chans),
            whole_block((1, chans)),
            tile(chans),
            whole_block((1, chans)),
        ],
        out_specs=[tile(chans), tile(128)],
        out_shape=[
            jax.ShapeDtypeStruct((2, rows, chans), BF16),
            jax.ShapeDtypeStruct((2, rows, 128), F32),
        ],
        compiler_params=params(2),
        name="gate",
    )(y_in, x_conv, bc_conv, state, grown, skip, z_val, gain)


def local(
    tokens,
    w_xz,
    w_bc,
    conv_x,
    conv_bc,
    tail_x,
    tail_bc,
    decay_code,
    skip_gain,
    state_in,
    norm_gain,
    w_out,
):
    rows = tokens.shape[0]
    all_heads, head_dim, nstate = state_in.shape
    seq_count = lax.axis_size("seq")
    head_count = lax.axis_size("head")
    inner = all_heads * head_dim * head_count
    me = lax.axis_index("seq")
    mine = lax.axis_index("head")
    half = (me // PAIR) % 2
    heads = all_heads // 2
    chans = heads * head_dim
    depth = w_xz.shape[0]

    share = tokens.shape[1] // head_count
    quarters = {0: swapped(cut(tokens, mine, share, 1), "seq", PAIR)}
    before = shifted(tokens[rows - HALO :], "seq", 1)
    before_other = swapped(before, "seq", PAIR)
    bit = head_count // 2
    while bit >= 1:
        for mask in list(quarters):
            quarters[mask | bit] = swapped(quarters[mask], "head", bit)
        bit //= 2
    own = jnp.concatenate([before, before_other, tokens], axis=0)
    others = jnp.stack([quarters[mask] for mask in range(head_count)])

    flat_w = lax.optimization_barrier(w_xz.reshape(depth, -1))
    full = flat_w.shape[1] // 2
    x_w, z_w = flat_w[:, :full], flat_w[:, full:]
    x_pieces = spread(cut(x_w, half, chans, 1), cut(x_w, 1 - half, chans, 1), seq_count)
    z_pieces = spread(cut(z_w, half, chans, 1), cut(z_w, 1 - half, chans, 1), seq_count, x_pieces)
    out_pieces = spread(cut(w_out, half, chans, 0), cut(w_out, 1 - half, chans, 0), seq_count, z_pieces)

    narrow = w_bc.shape[1] // head_count
    pack = max(1, 128 // narrow)
    some = cut(w_bc, mine, narrow, 1).reshape(pack, depth // pack, narrow)
    some = some.transpose(1, 0, 2).reshape(1, depth // pack, pack * narrow)
    bit = 1
    while bit < seq_count:
        some = natural(some, "seq", bit, 0)
        bit *= 2
    some = some.reshape(seq_count, depth // pack, pack, narrow).transpose(0, 2, 1, 3)
    bc_own = dot(own, some.reshape(-1, narrow)).astype(BF16)
    bit = 1
    while bit < head_count:
        bc_own = natural(bc_own, "head", bit, 1)
        bit *= 2
    bc_other = swapped(bc_own[2 * HALO :], "seq", PAIR)

    logdec = -decay_code.astype(F32) / (16.0 * rows * seq_count)
    ld_own = cut(logdec, half, heads, 1)
    ld = jnp.stack([ld_own, swapped(cut(logdec, 1 - half, heads, 1), "seq", PAIR)])
    blocks = rows // Q
    cum = jnp.cumsum(ld.reshape(2, blocks, Q, heads), axis=2)
    cumt = cum.transpose(0, 1, 3, 2)
    ends = cum[:, :, -1:, :]
    remaining = jnp.repeat(jnp.exp(ends - cum).reshape(2, rows, heads), head_dim, axis=2)
    block_decay = jnp.repeat(jnp.exp(ends), head_dim, axis=3)
    cum = cum.reshape(2, rows, heads)
    grown = jnp.repeat(jnp.exp(cum), head_dim, axis=2)
    totals = jnp.sum(ld, axis=1)
    masks = [0, PAIR]
    bit = 1
    while bit < seq_count:
        if bit != PAIR:
            totals = jnp.concatenate([totals, swapped(totals, "seq", bit)])
            masks = masks + [m | bit for m in masks]
        bit *= 2
    places = me ^ jnp.array(masks, jnp.int32)

    def decay_between(low, high):
        chosen = jnp.where((places >= low) & (places < high), 1.0, 0.0)[:, None]
        return jnp.repeat(jnp.exp(jnp.sum(chosen * totals, axis=0)), head_dim)[None, :]

    def own_part(mask):
        return cut(own, me ^ mask, depth, 1)

    def other_part(mask):
        start = (me ^ mask) * depth
        return lax.dynamic_slice(others, (start // share ^ mine, 0, start % share), (1, rows, depth))[0]

    def project(pieces, part):
        total = None
        for mask, piece in pieces.items():
            term = dot(part(mask), piece)
            total = term if total is None else total + term
        return total.astype(BF16)

    x_own = project(x_pieces, own_part)
    x_other = project(x_pieces, other_part)
    z_own = project(z_pieces, lambda mask: own_part(mask)[2 * HALO :])
    z_other = project(z_pieces, other_part)

    ranges = [me, me ^ PAIR]
    first = jnp.stack([(r == 0).astype(jnp.int32) for r in ranges])

    def padded(tail):
        return jnp.pad(tail, ((HALO - tail.shape[0], 0), (0, 0)))

    x_conv, bc_conv, added = front(
        first,
        x_own,
        x_other,
        bc_own,
        bc_other,
        padded(cut(tail_x, half, chans, 1)),
        padded(tail_bc),
        cut(conv_x, half, chans, 1),
        conv_bc,
        remaining,
    )

    inside = [jnp.zeros_like(added[:, 0])]
    for b in range(blocks):
        inside.append(block_decay[:, b] * inside[-1] + added[:, b])
    ending = inside.pop()

    group = 4
    across = swapped(ending.astype(BF16), "seq", 1).astype(F32)
    ended = {0: ending[0], PAIR: ending[1], 1: across[0], PAIR | 1: across[1]}
    base = (me // group) * group
    groups = seq_count // group
    total = 0.0
    for mask, value in ended.items():
        total = total + decay_between((me ^ mask) + 1, base + group) * value
    carry = shifted(total.astype(BF16), "seq", group).astype(F32)
    covered = 1
    while covered < groups - 1:
        more = shifted(carry.astype(BF16), "seq", group * covered).astype(F32)
        carry = carry + decay_between(base - group * covered, base) * more
        covered *= 2
    begin = cut(state_in, half, heads, 0).transpose(2, 0, 1).reshape(nstate, chans)
    incoming = []
    for place in ranges:
        value = decay_between(0, place) * begin + decay_between(base, place) * carry
        for mask, ended_value in ended.items():
            scale = jnp.where((me ^ mask) < place, decay_between((me ^ mask) + 1, place), 0.0)
            value = value + scale * ended_value
        incoming.append(value)
    opening = jnp.stack(incoming)
    states = []
    for b in range(blocks):
        states.append(opening + inside[b])
        opening = block_decay[:, b] * opening

    y_in = intra(x_conv, bc_conv, cum, cumt, heads)
    gated, squares = gate(
        y_in,
        x_conv,
        bc_conv,
        jnp.stack(states, axis=1),
        grown,
        jnp.repeat(cut(skip_gain, half, heads, 0), head_dim)[None, :],
        jnp.stack([z_own, z_other]),
        cut(norm_gain, half, chans, 0)[None, :],
    )

    squares = squares[0, :, 0] + swapped(squares[1, :, 0], "seq", PAIR)
    bit = 1
    while bit < head_count:
        squares = squares + swapped(squares, "head", bit)
        bit *= 2
    scale = lax.rsqrt(squares / inner + 1e-05)[:, None]

    per = seq_count // head_count
    relation = (me // per) ^ mine

    def by_destination(low):
        return by_xor([out_pieces[q * per + low] for q in range(head_count)], relation)

    def fold_head(parts):
        bit = 1
        while bit < head_count:
            for r in list(parts):
                if r & bit:
                    got = swapped(parts.pop(r).astype(BF16), "head", bit)
                    parts[r ^ bit] = parts[r ^ bit] + got.astype(F32)
            bit *= 2
        return parts[0]

    def fold_core(weights, value):
        sent = {r: swapped(dot(value, w).astype(BF16), "head", 1) for r, w in enumerate(weights) if r & 1}
        return {r: dot(value, w) + sent[r | 1].astype(F32) for r, w in enumerate(weights) if not r & 1}

    def fold_pair(mine_part, other_part):
        return mine_part + swapped(other_part.astype(BF16), "seq", PAIR).astype(F32)

    flat = gated.reshape(2 * rows, chans)
    done = {}
    for low in range(0, per, 2):
        whole = fold_head(fold_core(by_destination(low), flat))
        done[low] = fold_pair(whole[:rows], whole[rows:])
    for low in range(1, per, 2):
        weights = by_destination(low)
        away = fold_core(weights, gated[1])
        here = fold_core(weights, gated[0])
        done[low] = fold_head({r: fold_pair(here[r], away[r]) for r in here})
    result = by_xor([done[low] for low in range(per)], me % per)
    return jnp.concatenate([(piece * scale).astype(BF16) for piece in result], axis=1)


def solution(mesh):
    return jax.shard_map(
        local,
        mesh=mesh,
        in_specs=(
            P("seq", None),
            P("seq", None, "head"),
            P("seq", None),
            P(None, "head"),
            P(),
            P(None, "head"),
            P(),
            P("seq", "head"),
            P("head"),
            P("head", None, None),
            P("head"),
            P("head", "seq"),
        ),
        out_specs=P("seq", "head"),
        check_vma=False,
    )
```

```python
import functools

import jax
import jax.numpy as jnp
from jax import lax
from jax.experimental import pallas as pl
from jax.experimental.pallas import tpu as pltpu
from jax.sharding import PartitionSpec as P

Q = 256
HALO = 16
PAIR = 2
F32 = jnp.float32
BF16 = jnp.bfloat16
VMEM_LIMIT = 48 * 1024 * 1024


def swapped(value, axis, bit):
    size = lax.axis_size(axis)
    return lax.ppermute(value, axis, [(i, i ^ bit) for i in range(size)])


def shifted(value, axis, by):
    size = lax.axis_size(axis)
    return lax.ppermute(value, axis, [(i, i + by) for i in range(size - by)])


def cut(value, index, size, axis):
    return lax.dynamic_slice_in_dim(value, index * size, size, axis)


def after(value, *others):
    return lax.optimization_barrier((value, *others))[0]


def spread(own, other, seq_count, gates):
    bits = [1 << b for b in range(seq_count.bit_length() - 1)]
    bits = [b for b in bits if b > PAIR] + [b for b in bits if b < PAIR]
    pair_gate, high_gate, low_gate = gates
    if pair_gate is not None:
        other = after(other, pair_gate)
    pieces = {0: own, PAIR: swapped(other, "seq", PAIR)}
    for bit in bits:
        for mask in list(pieces):
            value = pieces[mask]
            gate = high_gate if bit > PAIR else low_gate
            if mask == 0 and gate is not None:
                value = after(value, gate)
            pieces[mask | bit] = swapped(value, "seq", bit)
    return pieces


def natural(value, axis_name, bit, axis):
    other = swapped(value, axis_name, bit)
    low = (lax.axis_index(axis_name) & bit) == 0
    return jnp.where(
        low, jnp.concatenate([value, other], axis=axis), jnp.concatenate([other, value], axis=axis)
    )


def by_xor(values, index):
    bit = 1
    while bit < len(values):
        flip = (index & bit) != 0
        values = [jnp.where(flip, values[j ^ bit], values[j]) for j in range(len(values))]
        bit *= 2
    return values


def dot(a, b):
    return jnp.dot(a, b, preferred_element_type=F32)


def front_kernel(
    first_ref, xo_ref, xp_ref, bo_ref, bp_ref, tx_ref, tbc_ref, kx_ref, kbc_ref, dec_ref, xc_ref, bcc_ref, f_ref
):
    rows = xc_ref.shape[1]
    for r in range(2):
        is_first = first_ref[r] == 1

        def conv(own_ref, other_ref, tail_ref, k_ref):
            halo = other_ref[r * HALO : (r + 1) * HALO].astype(F32)
            halo = jnp.where(is_first, tail_ref[...].astype(F32), halo)
            body = (own_ref[...] if r == 0 else other_ref[2 * HALO :]).astype(F32)
            whole = jnp.concatenate([halo, body], axis=0)
            taps = k_ref.shape[0]
            total = jnp.zeros(body.shape, F32)
            for k in range(taps):
                start = HALO - (taps - 1) + k
                total = total + k_ref[k : k + 1, :] * whole[start : start + rows]
            return (total * jax.nn.sigmoid(total)).astype(BF16)

        x_val = conv(xo_ref, xp_ref, tx_ref, kx_ref)
        bc_val = conv(bo_ref, bp_ref, tbc_ref, kbc_ref)
        xc_ref[r] = x_val
        bcc_ref[r] = bc_val
        decayed = (x_val.astype(F32) * dec_ref[r]).astype(BF16)
        nstate = bc_val.shape[1] // 2
        for start in range(0, rows, Q):
            f_ref[r, start // Q] = lax.dot_general(
                bc_val[start : start + Q, :nstate],
                decayed[start : start + Q],
                (((0,), (0,)), ((), ())),
                preferred_element_type=F32,
            )


def intra_kernel(heads, x_ref, bc_ref, cum_ref, cumt_ref, y_ref):
    nstate = bc_ref.shape[2] // 2
    span = x_ref.shape[1]
    head_dim = x_ref.shape[2] // heads
    b_val = bc_ref[0, :, :nstate]
    c_val = bc_ref[0, :, nstate:]
    scores = lax.dot_general(c_val, b_val, (((1,), (1,)), ((), ())), preferred_element_type=F32)
    lower = lax.broadcasted_iota(jnp.int32, (span, span), 0) >= lax.broadcasted_iota(jnp.int32, (span, span), 1)
    scores = jnp.where(lower, scores, 0.0)
    pair = 128 // head_dim
    for start in range(0, heads, pair):
        outs = []
        for h in range(start, start + pair):
            diff = cum_ref[0, :, h : h + 1] - cumt_ref[0, 0, h : h + 1, :]
            weights = (jnp.exp(jnp.where(lower, diff, 0.0)) * scores).astype(BF16)
            outs.append(dot(weights, x_ref[0, :, h * head_dim : (h + 1) * head_dim]))
        y_ref[0, :, start * head_dim : (start + pair) * head_dim] = jnp.concatenate(outs, axis=1)


def gate_kernel(y_ref, x_ref, bc_ref, st_ref, e_ref, skip_ref, z_ref, gain_ref, g_ref, ss_ref):
    nstate = st_ref.shape[2]
    c_val = bc_ref[0, :, nstate:]
    state = st_ref[0, 0]
    high = state.astype(BF16)
    low = (state - high.astype(F32)).astype(BF16)
    carried = dot(c_val, high) + dot(c_val, low)
    y_val = (y_ref[0] + e_ref[0] * carried) / nstate + skip_ref[...] * x_ref[0].astype(F32)
    z_val = z_ref[0].astype(F32)
    gated = y_val * (z_val * jax.nn.sigmoid(z_val))
    g_ref[0] = (gated * gain_ref[...]).astype(BF16)
    total = jnp.sum(gated * gated, axis=1, keepdims=True)
    ss_ref[0] = jnp.broadcast_to(total, ss_ref.shape[1:])


def params(grid):
    return pltpu.CompilerParams(dimension_semantics=("arbitrary",) * grid, vmem_limit_bytes=VMEM_LIMIT)


def whole_block(shape):
    return pl.BlockSpec(shape, lambda *_: (0,) * len(shape))


def front(first, x_own, x_other, bc_own, bc_other, tail_x, tail_bc, conv_x, conv_bc, decay):
    rows, chans = x_own.shape
    bcw = bc_own.shape[1]
    return pl.pallas_call(
        front_kernel,
        in_specs=[pl.BlockSpec(memory_space=pltpu.SMEM)] + [pl.BlockSpec(memory_space=pltpu.VMEM)] * 9,
        out_specs=[pl.BlockSpec(memory_space=pltpu.VMEM)] * 3,
        out_shape=[
            jax.ShapeDtypeStruct((2, rows, chans), BF16),
            jax.ShapeDtypeStruct((2, rows, bcw), BF16),
            jax.ShapeDtypeStruct((2, rows // Q, bcw // 2, chans), F32),
        ],
        compiler_params=pltpu.CompilerParams(vmem_limit_bytes=VMEM_LIMIT),
        name="front",
    )(first, x_own, x_other, bc_own, bc_other, tail_x, tail_bc, conv_x, conv_bc, decay)


def project_kernel(place_ref, others_ref, *refs):
    pieces, out_ref = refs[:-1], refs[-1]
    depth = pieces[0].shape[0]
    total = None
    for k, piece in enumerate(pieces):
        start = pl.multiple_of(place_ref[1, k], depth)
        term = dot(others_ref[place_ref[0, k], :, pl.ds(start, depth)], piece[...])
        total = term if total is None else total + term
    out_ref[...] = total.astype(BF16)


def project_others(places, others, pieces):
    rows = others.shape[1]
    chans = pieces[0].shape[1]
    return pl.pallas_call(
        project_kernel,
        in_specs=[pl.BlockSpec(memory_space=pltpu.SMEM)]
        + [pl.BlockSpec(memory_space=pltpu.VMEM)] * (1 + len(pieces)),
        out_specs=pl.BlockSpec(memory_space=pltpu.VMEM),
        out_shape=jax.ShapeDtypeStruct((rows, chans), BF16),
        compiler_params=pltpu.CompilerParams(vmem_limit_bytes=VMEM_LIMIT),
        name="project",
    )(places, others, *pieces)


def intra(x_conv, bc_conv, cum, cumt, heads):
    _, rows, chans = x_conv.shape
    bcw = bc_conv.shape[2]
    blocks = rows // Q

    def tile(w):
        return pl.BlockSpec((1, Q, w), lambda r, i: (r, i, 0))

    work = 2 * rows * Q
    return pl.pallas_call(
        functools.partial(intra_kernel, heads),
        grid=(2, blocks),
        in_specs=[tile(chans), tile(bcw), tile(heads), pl.BlockSpec((1, 1, heads, Q), lambda r, i: (r, i, 0, 0))],
        out_specs=tile(chans),
        out_shape=jax.ShapeDtypeStruct((2, rows, chans), F32),
        compiler_params=params(2),
        cost_estimate=pl.CostEstimate(
            flops=2 * work * (chans + bcw // 2), bytes_accessed=12 * rows * chans, transcendentals=work * heads
        ),
        name="intra",
    )(x_conv, bc_conv, cum, cumt)


def gate(y_in, x_conv, bc_conv, state, grown, skip, z_val, gain):
    _, rows, chans = x_conv.shape
    bcw = bc_conv.shape[2]

    def tile(w):
        return pl.BlockSpec((1, Q, w), lambda r, i: (r, i, 0))

    return pl.pallas_call(
        gate_kernel,
        grid=(2, rows // Q),
        in_specs=[
            tile(chans),
            tile(chans),
            tile(bcw),
            pl.BlockSpec((1, 1, bcw // 2, chans), lambda r, i: (r, i, 0, 0)),
            tile(chans),
            whole_block((1, chans)),
            tile(chans),
            whole_block((1, chans)),
        ],
        out_specs=[tile(chans), tile(128)],
        out_shape=[
            jax.ShapeDtypeStruct((2, rows, chans), BF16),
            jax.ShapeDtypeStruct((2, rows, 128), F32),
        ],
        compiler_params=params(2),
        name="gate",
    )(y_in, x_conv, bc_conv, state, grown, skip, z_val, gain)


def local(
    tokens,
    w_xz,
    w_bc,
    conv_x,
    conv_bc,
    tail_x,
    tail_bc,
    decay_code,
    skip_gain,
    state_in,
    norm_gain,
    w_out,
):
    rows = tokens.shape[0]
    all_heads, head_dim, nstate = state_in.shape
    seq_count = lax.axis_size("seq")
    head_count = lax.axis_size("head")
    inner = all_heads * head_dim * head_count
    me = lax.axis_index("seq")
    mine = lax.axis_index("head")
    half = (me // PAIR) % 2
    heads = all_heads // 2
    chans = heads * head_dim
    depth = w_xz.shape[0]

    flat_w = lax.optimization_barrier(w_xz.reshape(depth, -1))
    full = flat_w.shape[1] // 2
    x_w, z_w = flat_w[:, :full], flat_w[:, full:]
    high = max(b for b in (PAIR, seq_count // 2))
    share = tokens.shape[1] // head_count
    quarters = {0: swapped(cut(tokens, mine, share, 1), "seq", PAIR)}
    x_pieces = spread(
        cut(x_w, half, chans, 1), cut(x_w, 1 - half, chans, 1), seq_count, (None, None, None)
    )
    z_pieces = spread(
        cut(z_w, half, chans, 1),
        cut(z_w, 1 - half, chans, 1),
        seq_count,
        (quarters[0], x_pieces[high], x_pieces[PAIR | 1]),
    )
    out_pieces = spread(
        cut(w_out, half, chans, 0),
        cut(w_out, 1 - half, chans, 0),
        seq_count,
        (z_pieces[PAIR], z_pieces[high], z_pieces[PAIR | 1]),
    )

    bit = head_count // 2
    while bit >= 1:
        for mask in list(quarters):
            quarters[mask | bit] = swapped(quarters[mask], "head", bit)
        bit //= 2
    before = shifted(tokens[rows - HALO :], "seq", 1)
    before_other = swapped(after(before, x_pieces[PAIR]), "seq", PAIR)
    halo = after(jnp.concatenate([before, before_other], axis=0), x_pieces[high])
    others = jnp.stack(
        [
            jnp.concatenate([cut(halo, mine ^ mask, share, 1), quarters[mask]], axis=0)
            for mask in range(head_count)
        ]
    )

    narrow = w_bc.shape[1] // head_count
    pack = max(1, 128 // narrow)
    some = cut(w_bc, mine, narrow, 1).reshape(pack, depth // pack, narrow)
    some = some.transpose(1, 0, 2).reshape(depth // pack, pack * narrow)
    some = after(lax.all_gather(some, "seq", axis=0), x_pieces[high])
    some = some.reshape(seq_count, depth // pack, pack, narrow).transpose(0, 2, 1, 3)
    some = some.reshape(-1, narrow)
    bc_part = jnp.concatenate([dot(halo, some), dot(tokens, some)], axis=0).astype(BF16)
    bit = 1
    while bit < head_count:
        bc_part = natural(bc_part, "head", bit, 1)
        bit *= 2
    bc_own = bc_part[2 * HALO :]
    bc_other = jnp.concatenate([bc_part[: 2 * HALO], swapped(bc_own, "seq", PAIR)], axis=0)

    logdec = -decay_code.T.astype(F32) / (16.0 * rows * seq_count)
    ld_other = swapped(cut(logdec, 1 - half, heads, 0), "seq", PAIR)
    ld = jnp.stack([cut(logdec, half, heads, 0), after(ld_other, x_pieces[PAIR])])
    blocks = rows // Q
    cumt = jnp.cumsum(ld.reshape(2, heads, blocks, Q), axis=3).transpose(0, 2, 1, 3)
    cum = cumt.transpose(0, 1, 3, 2)
    ends = cum[:, :, -1:, :]
    remaining = jnp.repeat(jnp.exp(ends - cum).reshape(2, rows, heads), head_dim, axis=2)
    block_decay = jnp.repeat(jnp.exp(ends), head_dim, axis=3)
    cum = cum.reshape(2, rows, heads)
    grown = jnp.repeat(jnp.exp(cum), head_dim, axis=2)
    totals = jnp.sum(ld, axis=2)
    masks = [0, PAIR]
    bit = 1
    while bit < seq_count:
        if bit != PAIR:
            got = after(swapped(totals, "seq", bit), x_pieces[high])
            totals = jnp.concatenate([totals, got])
            masks = masks + [m | bit for m in masks]
        bit *= 2
    places = me ^ jnp.array(masks, jnp.int32)

    def decay_between(low, high):
        chosen = jnp.where((places >= low) & (places < high), 1.0, 0.0)[:, None]
        return jnp.repeat(jnp.exp(jnp.sum(chosen * totals, axis=0)), head_dim)[None, :]

    def own_part(mask):
        return cut(tokens, me ^ mask, depth, 1)

    def other_place(mask):
        start = (me ^ mask) * depth
        return start // share ^ mine, start % share

    def other_part(mask):
        block, start = other_place(mask)
        return lax.dynamic_slice(others, (block, 2 * HALO, start), (1, rows, depth))[0]

    def project(pieces, part):
        total = None
        for mask, piece in pieces.items():
            term = dot(part(mask), piece)
            total = term if total is None else total + term
        return total.astype(BF16)

    x_own = project(x_pieces, own_part)
    spots = [other_place(mask) for mask in x_pieces]
    spots = jnp.stack([jnp.stack([jnp.int32(p[i]) for p in spots]) for i in range(2)])
    x_other = project_others(spots, others, list(x_pieces.values()))
    z_own = project(z_pieces, own_part)
    z_other = project(z_pieces, other_part)

    ranges = [me, me ^ PAIR]
    first = jnp.stack([(r == 0).astype(jnp.int32) for r in ranges])

    def padded(tail):
        return jnp.pad(tail, ((HALO - tail.shape[0], 0), (0, 0)))

    x_conv, bc_conv, added = front(
        first,
        x_own,
        x_other,
        bc_own,
        bc_other,
        padded(cut(tail_x, half, chans, 1)),
        padded(tail_bc),
        cut(conv_x, half, chans, 1),
        conv_bc,
        remaining,
    )

    inside = [jnp.zeros_like(added[:, 0])]
    for b in range(blocks):
        inside.append(block_decay[:, b] * inside[-1] + added[:, b])
    ending = inside.pop()

    group = 4
    across = swapped(ending.astype(BF16), "seq", 1).astype(F32)
    ended = {0: ending[0], PAIR: ending[1], 1: across[0], PAIR | 1: across[1]}
    base = (me // group) * group
    groups = seq_count // group
    total = 0.0
    for mask, value in ended.items():
        total = total + decay_between((me ^ mask) + 1, base + group) * value
    carry = shifted(total.astype(BF16), "seq", group).astype(F32)
    covered = 1
    while covered < groups - 1:
        more = shifted(carry.astype(BF16), "seq", group * covered).astype(F32)
        carry = carry + decay_between(base - group * covered, base) * more
        covered *= 2
    begin = cut(state_in, half, heads, 0).transpose(2, 0, 1).reshape(nstate, chans)
    incoming = []
    for place in ranges:
        value = decay_between(0, place) * begin + decay_between(base, place) * carry
        for mask, ended_value in ended.items():
            scale = jnp.where((me ^ mask) < place, decay_between((me ^ mask) + 1, place), 0.0)
            value = value + scale * ended_value
        incoming.append(value)
    opening = jnp.stack(incoming)
    states = []
    for b in range(blocks):
        states.append(opening + inside[b])
        opening = block_decay[:, b] * opening

    y_in = intra(x_conv, bc_conv, cum, cumt, heads)
    gated, squares = gate(
        y_in,
        x_conv,
        bc_conv,
        jnp.stack(states, axis=1),
        grown,
        jnp.repeat(cut(skip_gain, half, heads, 0), head_dim)[None, :],
        jnp.stack([z_own, z_other]),
        cut(norm_gain, half, chans, 0)[None, :],
    )

    per = seq_count // head_count
    relation = (me // per) ^ mine
    flat = gated.reshape(2 * rows, chans)

    def by_destination(low):
        return by_xor([out_pieces[q * per + low] for q in range(head_count)], relation)

    def send_far(weights):
        far = jnp.concatenate(weights[1::2], axis=1)
        return swapped(dot(flat, far).astype(BF16), "head", 1).astype(F32)

    def fold_head(parts):
        bit = 2
        while len(parts) > 1:
            sent = jnp.concatenate(parts[1::2], axis=1) if len(parts) > 2 else parts[1]
            got = swapped(sent.astype(BF16), "head", bit).astype(F32)
            parts = columns_added(parts[::2], got)
            bit *= 2
        return parts[0]

    def columns_added(parts, got):
        width = parts[0].shape[1]
        return [part + got[:, i * width : (i + 1) * width] for i, part in enumerate(parts)]

    def swap_pair(value):
        return swapped(value.astype(BF16), "seq", PAIR).astype(F32)

    done = {}
    lows = {low: by_destination(low) for low in range(per)}
    got_far = {low: send_far(lows[low]) for low in range(per)}
    for low in range(0, per, 2):
        parts = columns_added([dot(flat, w) for w in lows[low][::2]], got_far[low])
        whole = fold_head(parts)
        done[low] = whole[:rows] + swap_pair(whole[rows:])
    for low in range(1, per, 2):
        near = lows[low][::2]
        away = swap_pair(dot(gated[1], jnp.concatenate(near, axis=1)) + got_far[low][rows:])
        here = columns_added([dot(gated[0], w) for w in near], got_far[low][:rows])
        done[low] = fold_head(columns_added(here, away))

    squares = after(squares[:, :, 0], got_far[per - 1])
    squares = squares[0] + swapped(squares[1], "seq", PAIR)
    bit = 1
    while bit < head_count:
        squares = squares + swapped(squares, "head", bit)
        bit *= 2
    scale = lax.rsqrt(squares / inner + 1e-05)[:, None]
    result = by_xor([done[low] for low in range(per)], me % per)
    return jnp.concatenate([(piece * scale).astype(BF16) for piece in result], axis=1)


def solution(mesh):
    return jax.shard_map(
        local,
        mesh=mesh,
        in_specs=(
            P("seq", None),
            P("seq", None, "head"),
            P("seq", None),
            P(None, "head"),
            P(),
            P(None, "head"),
            P(),
            P("seq", "head"),
            P("head"),
            P("head", None, None),
            P("head"),
            P("head", "seq"),
        ),
        out_specs=P("seq", "head"),
        check_vma=False,
    )
```

```python
import functools

import jax
import jax.numpy as jnp
from jax import lax
from jax.experimental import pallas as pl
from jax.experimental.pallas import tpu as pltpu
from jax.sharding import PartitionSpec as P

Q = 256
HALO = 16
PAIR = 2
F32 = jnp.float32
BF16 = jnp.bfloat16
VMEM_LIMIT = 48 * 1024 * 1024
LIGHT = pl.CostEstimate(flops=1, bytes_accessed=1, transcendentals=0)


def swapped(value, axis, bit):
    size = lax.axis_size(axis)
    return lax.ppermute(value, axis, [(i, i ^ bit) for i in range(size)])


def shifted(value, axis, by):
    size = lax.axis_size(axis)
    return lax.ppermute(value, axis, [(i, i + by) for i in range(size - by)])


def cut(value, index, size, axis):
    return lax.dynamic_slice_in_dim(value, index * size, size, axis)


def after(value, *others):
    return lax.optimization_barrier((value, *others))[0]


ROUNDS = (
    (("x", 4), ("x", 6), ("x", 3), ("x", 5), ("t", 0)),
    (("z", 4), ("z", 2), ("x", 7), ("z", 1), ("t", 1)),
    (("z", 6), ("z", 3), ("z", 5), ("w", 2), ("t", 2)),
    (("w", 4), ("z", 7), ("w", 1)),
    (("w", 6), ("w", 3), ("w", 5)),
)
WAITS = {send: ROUNDS[i] for i in range(len(ROUNDS) - 1) for send in ROUNDS[i + 1]}
WAITS[("t", 0)] = (("x", 2),)


class Sends:
    def __init__(self, own, given, quarter):
        self.own, self.given, self.quarter = own, given, quarter
        self.made = {}

    def get(self, kind, mask):
        name = (kind, mask)
        if name not in self.made:
            self.made[name] = self.tokens(mask) if kind == "t" else self.piece(kind, mask)
        return self.made[name]

    def waiting(self, name, value):
        others = [self.get(*other) for other in WAITS.get(name, ())]
        return after(value, *others) if others else value

    def piece(self, kind, mask):
        if mask == 0:
            return self.own[kind]
        if mask == PAIR:
            bit, value = PAIR, self.given[kind]
        else:
            bit = 1 if mask & 1 else 1 << (mask.bit_length() - 1)
            value = self.get(kind, mask ^ bit)
        return swapped(self.waiting((kind, mask), value), "seq", bit)

    def tokens(self, step):
        if step == 0:
            return swapped(self.waiting(("t", 0), self.quarter), "seq", PAIR)
        if step == 1:
            value = self.get("t", 0)[None]
            bit = lax.axis_size("head") // 2
            while bit > 1:
                got = swapped(self.waiting(("t", 1), value), "head", bit)
                value = jnp.concatenate([value, got])
                bit //= 2
            return value
        return swapped(self.waiting(("t", 2), self.get("t", 1)), "head", 1)


def natural(value, axis_name, bit, axis):
    other = swapped(value, axis_name, bit)
    low = (lax.axis_index(axis_name) & bit) == 0
    return jnp.where(
        low, jnp.concatenate([value, other], axis=axis), jnp.concatenate([other, value], axis=axis)
    )


def by_xor(values, index):
    bit = 1
    while bit < len(values):
        flip = (index & bit) != 0
        values = [jnp.where(flip, values[j ^ bit], values[j]) for j in range(len(values))]
        bit *= 2
    return values


def dot(a, b):
    return jnp.dot(a, b, preferred_element_type=F32)


def front_kernel(
    first_ref, x_ref, bc_ref, tx_ref, tbc_ref, kx_ref, kbc_ref, dec_ref, xc_ref, bcc_ref, f_ref
):
    rows = xc_ref.shape[1]
    for r in range(2):
        is_first = first_ref[r] == 1

        def conv(pre_ref, tail_ref, k_ref):
            halo = jnp.where(is_first, tail_ref[...].astype(F32), pre_ref[r, :HALO].astype(F32))
            body = pre_ref[r, HALO:].astype(F32)
            whole = jnp.concatenate([halo, body], axis=0)
            taps = k_ref.shape[0]
            total = jnp.zeros(body.shape, F32)
            for k in range(taps):
                start = HALO - (taps - 1) + k
                total = total + k_ref[k : k + 1, :] * whole[start : start + rows]
            return (total * jax.nn.sigmoid(total)).astype(BF16)

        x_val = conv(x_ref, tx_ref, kx_ref)
        bc_val = conv(bc_ref, tbc_ref, kbc_ref)
        xc_ref[r] = x_val
        bcc_ref[r] = bc_val
        decayed = (x_val.astype(F32) * dec_ref[r]).astype(BF16)
        nstate = bc_val.shape[1] // 2
        for start in range(0, rows, Q):
            f_ref[r, start // Q] = lax.dot_general(
                bc_val[start : start + Q, :nstate],
                decayed[start : start + Q],
                (((0,), (0,)), ((), ())),
                preferred_element_type=F32,
            )


def intra_kernel(heads, x_ref, bc_ref, cum_ref, cumt_ref, y_ref):
    nstate = bc_ref.shape[2] // 2
    span = x_ref.shape[1]
    head_dim = x_ref.shape[2] // heads
    b_val = bc_ref[0, :, :nstate]
    c_val = bc_ref[0, :, nstate:]
    scores = lax.dot_general(c_val, b_val, (((1,), (1,)), ((), ())), preferred_element_type=F32)
    lower = lax.broadcasted_iota(jnp.int32, (span, span), 0) >= lax.broadcasted_iota(jnp.int32, (span, span), 1)
    scores = jnp.where(lower, scores, 0.0)
    pair = 128 // head_dim
    for start in range(0, heads, pair):
        outs = []
        for h in range(start, start + pair):
            diff = cum_ref[0, :, h : h + 1] - cumt_ref[0, 0, h : h + 1, :]
            weights = (jnp.exp(jnp.where(lower, diff, 0.0)) * scores).astype(BF16)
            outs.append(dot(weights, x_ref[0, :, h * head_dim : (h + 1) * head_dim]))
        y_ref[0, :, start * head_dim : (start + pair) * head_dim] = jnp.concatenate(outs, axis=1)


def gate_kernel(y_ref, x_ref, bc_ref, st_ref, e_ref, skip_ref, z_ref, gain_ref, g_ref, ss_ref):
    nstate = st_ref.shape[2]
    c_val = bc_ref[0, :, nstate:]
    state = st_ref[0, 0]
    high = state.astype(BF16)
    low = (state - high.astype(F32)).astype(BF16)
    carried = dot(c_val, high) + dot(c_val, low)
    y_val = (y_ref[0] + e_ref[0] * carried) / nstate + skip_ref[...] * x_ref[0].astype(F32)
    z_val = z_ref[0].astype(F32)
    gated = y_val * (z_val * jax.nn.sigmoid(z_val))
    g_ref[0] = (gated * gain_ref[...]).astype(BF16)
    total = jnp.sum(gated * gated, axis=1, keepdims=True)
    ss_ref[0] = jnp.broadcast_to(total, ss_ref.shape[1:])


def params(grid):
    return pltpu.CompilerParams(dimension_semantics=("arbitrary",) * grid, vmem_limit_bytes=VMEM_LIMIT)


def whole_block(shape):
    return pl.BlockSpec(shape, lambda *_: (0,) * len(shape))


def front(first, x_pre, bc_pre, tail_x, tail_bc, conv_x, conv_bc, decay):
    rows, chans = x_pre.shape[1] - HALO, x_pre.shape[2]
    bcw = bc_pre.shape[2]
    return pl.pallas_call(
        front_kernel,
        in_specs=[pl.BlockSpec(memory_space=pltpu.SMEM)] + [pl.BlockSpec(memory_space=pltpu.VMEM)] * 7,
        out_specs=[pl.BlockSpec(memory_space=pltpu.VMEM)] * 3,
        out_shape=[
            jax.ShapeDtypeStruct((2, rows, chans), BF16),
            jax.ShapeDtypeStruct((2, rows, bcw), BF16),
            jax.ShapeDtypeStruct((2, rows // Q, bcw // 2, chans), F32),
        ],
        compiler_params=pltpu.CompilerParams(vmem_limit_bytes=VMEM_LIMIT),
        cost_estimate=LIGHT,
        name="front",
    )(first, x_pre, bc_pre, tail_x, tail_bc, conv_x, conv_bc, decay)


def project_kernel(depth, with_halo, one_weight, place_ref, *refs):
    refs = list(refs)
    out_ref = refs.pop()
    halo_ref = refs.pop(0) if with_halo else None
    tokens_ref, others_ref = refs[:2]
    rows = tokens_ref.shape[0]
    lead = HALO if with_halo else 0
    totals = [None] * 3
    for k in range(place_ref.shape[1]):
        start = pl.multiple_of(place_ref[0, k], depth)
        place = pl.multiple_of(place_ref[2, k], depth)
        weight = refs[2][pl.ds(start, depth), :] if one_weight else refs[2 + k][:depth]
        lefts = [tokens_ref[:, pl.ds(start, depth)], others_ref[place_ref[1, k], :rows, pl.ds(place, depth)]]
        if with_halo:
            lefts.append(halo_ref[:, pl.ds(start, depth)])
        for i, left in enumerate(lefts):
            term = dot(left, weight)
            totals[i] = term if totals[i] is None else totals[i] + term
    for r in range(2):
        out_ref[r, lead:] = totals[r].astype(BF16)
        if with_halo:
            out_ref[r, :lead] = totals[2][r * HALO : (r + 1) * HALO].astype(BF16)


def project(places, depth, tokens, others, weights, halo=None):
    rows = tokens.shape[0] + (0 if halo is None else HALO)
    chans = weights[0].shape[1]
    operands = ([] if halo is None else [halo]) + [tokens, others] + list(weights)
    return pl.pallas_call(
        functools.partial(project_kernel, depth, halo is not None, len(weights) == 1),
        in_specs=[pl.BlockSpec(memory_space=pltpu.SMEM)]
        + [pl.BlockSpec(memory_space=pltpu.VMEM)] * len(operands),
        out_specs=pl.BlockSpec(memory_space=pltpu.VMEM),
        out_shape=jax.ShapeDtypeStruct((2, rows, chans), BF16),
        compiler_params=pltpu.CompilerParams(vmem_limit_bytes=VMEM_LIMIT),
        cost_estimate=LIGHT,
        name="project",
    )(places, *operands)


def intra(x_conv, bc_conv, cum, cumt, heads):
    _, rows, chans = x_conv.shape
    bcw = bc_conv.shape[2]
    blocks = rows // Q

    def tile(w):
        return pl.BlockSpec((1, Q, w), lambda r, i: (r, i, 0))

    return pl.pallas_call(
        functools.partial(intra_kernel, heads),
        grid=(2, blocks),
        in_specs=[tile(chans), tile(bcw), tile(heads), pl.BlockSpec((1, 1, heads, Q), lambda r, i: (r, i, 0, 0))],
        out_specs=tile(chans),
        out_shape=jax.ShapeDtypeStruct((2, rows, chans), F32),
        compiler_params=params(2),
        cost_estimate=LIGHT,
        name="intra",
    )(x_conv, bc_conv, cum, cumt)


def gate(y_in, x_conv, bc_conv, state, grown, skip, z_val, gain):
    _, rows, chans = x_conv.shape
    bcw = bc_conv.shape[2]

    def tile(w):
        return pl.BlockSpec((1, Q, w), lambda r, i: (r, i, 0))

    return pl.pallas_call(
        gate_kernel,
        grid=(2, rows // Q),
        in_specs=[
            tile(chans),
            tile(chans),
            tile(bcw),
            pl.BlockSpec((1, 1, bcw // 2, chans), lambda r, i: (r, i, 0, 0)),
            tile(chans),
            whole_block((1, chans)),
            tile(chans),
            whole_block((1, chans)),
        ],
        out_specs=[tile(chans), tile(128)],
        out_shape=[
            jax.ShapeDtypeStruct((2, rows, chans), BF16),
            jax.ShapeDtypeStruct((2, rows, 128), F32),
        ],
        compiler_params=params(2),
        cost_estimate=LIGHT,
        name="gate",
    )(y_in, x_conv, bc_conv, state, grown, skip, z_val, gain)


def local(
    tokens,
    w_xz,
    w_bc,
    conv_x,
    conv_bc,
    tail_x,
    tail_bc,
    decay_code,
    skip_gain,
    state_in,
    norm_gain,
    w_out,
):
    rows = tokens.shape[0]
    all_heads, head_dim, nstate = state_in.shape
    seq_count = lax.axis_size("seq")
    head_count = lax.axis_size("head")
    inner = all_heads * head_dim * head_count
    me = lax.axis_index("seq")
    mine = lax.axis_index("head")
    half = (me // PAIR) % 2
    heads = all_heads // 2
    chans = heads * head_dim
    depth = w_xz.shape[0]

    lag = conv_x.shape[0] - 1
    code_sums = jnp.sum(decay_code, axis=0)
    digits = jnp.stack([(code_sums >> (8 * j)) & 255 for j in range(4)]).reshape(1, -1).astype(BF16)
    last_rows = tokens[rows - lag :].reshape(-1, chans)
    halo_rows = last_rows.shape[0]
    spare = -(halo_rows + 1) % 16
    extra = jnp.concatenate(
        [last_rows, jnp.pad(digits, ((0, spare), (0, chans - digits.shape[1])))], axis=0
    )

    share = tokens.shape[1] // head_count
    codes = decay_code.T
    given = cut(codes, 1 - half, heads, 0)
    given = jnp.stack([(given >> (8 * j)) & 255 for j in range(3)]).reshape(-1, share).astype(BF16)
    code_rows = given.shape[0]
    given = jnp.pad(given, ((0, -code_rows % 16), (0, 0)))

    flat_w = lax.optimization_barrier(w_xz.reshape(depth, -1))
    full = flat_w.shape[1] // 2
    x_w, z_w = flat_w[:, :full], flat_w[:, full:]
    high = max(b for b in (PAIR, seq_count // 2))
    own = {
        "x": jnp.concatenate([cut(x_w, half, chans, 1), extra], axis=0),
        "z": cut(z_w, half, chans, 1),
        "w": cut(w_out, half, chans, 0),
    }
    given_away = {
        "x": jnp.concatenate([cut(x_w, 1 - half, chans, 1), extra], axis=0),
        "z": cut(z_w, 1 - half, chans, 1),
        "w": cut(w_out, 1 - half, chans, 0),
    }
    sends = Sends(own, given_away, jnp.concatenate([cut(tokens, mine, share, 1), given], axis=0))
    masks = list(range(seq_count))
    x_pieces, z_pieces, out_pieces = [{mask: sends.get(kind, mask) for mask in masks} for kind in "xzw"]

    others = jnp.concatenate([sends.get("t", 1), sends.get("t", 2)])
    ranges = [me, me ^ PAIR]
    extras = jnp.stack([x_pieces[mask][depth:] for mask in range(seq_count)])

    def rows_before(place):
        got = lax.dynamic_index_in_dim(extras, (me ^ (place - 1)) & (seq_count - 1), 0, keepdims=False)
        return jnp.pad(got[:halo_rows].reshape(lag, -1), ((HALO - lag, 0), (0, 0)))

    halo = jnp.concatenate([rows_before(place) for place in ranges], axis=0)

    starts = [(me ^ mask) * depth for mask in masks]
    blocks = [a // share ^ mine for a in starts]
    blocks = [(b >> 1) + (b & 1) * (head_count // 2) for b in blocks]
    spots = [starts, blocks, [a % share for a in starts]]
    spots = jnp.stack([jnp.stack([jnp.int32(a) for a in row]) for row in spots])

    part = depth // head_count
    w_bc_all = lax.all_gather(cut(w_bc, mine, part, 0), ("seq", "head"), axis=0, tiled=True)
    bc_pre = project(spots, depth, tokens, others, [w_bc_all], halo)
    x_pre = project(spots, depth, tokens, others, list(x_pieces.values()), halo)
    z_val = project(spots, depth, tokens, others, list(z_pieces.values()))

    per_code = -1.0 / (16.0 * rows * seq_count)
    got = sends.get("t", 0)[rows : rows + code_rows].astype(F32).reshape(3, heads, rows)
    other_codes = got[0] + 256.0 * got[1] + 65536.0 * got[2]
    ld = jnp.stack([cut(codes, half, heads, 0).astype(F32), other_codes]) * per_code
    blocks = rows // Q
    cumt = jnp.cumsum(ld.reshape(2, heads, blocks, Q), axis=3).transpose(0, 2, 1, 3)
    cum = cumt.transpose(0, 1, 3, 2)
    ends = cum[:, :, -1:, :]
    remaining = jnp.repeat(jnp.exp(ends - cum).reshape(2, rows, heads), head_dim, axis=2)
    block_decay = jnp.repeat(jnp.exp(ends), head_dim, axis=3)
    cum = cum.reshape(2, rows, heads)
    grown = jnp.repeat(jnp.exp(cum), head_dim, axis=2)
    totals = jnp.stack([x_pieces[mask][depth + halo_rows] for mask in masks])
    totals = totals[:, : 4 * all_heads].astype(F32).reshape(-1, 4, all_heads)
    totals = sum(totals[:, j] * 256.0**j for j in range(4)) * per_code
    totals = cut(totals, half, heads, 1)
    places = me ^ jnp.array(masks, jnp.int32)

    def decay_between(low, high):
        chosen = jnp.where((places >= low) & (places < high), 1.0, 0.0)[:, None]
        return jnp.repeat(jnp.exp(jnp.sum(chosen * totals, axis=0)), head_dim)[None, :]

    first = jnp.stack([(r == 0).astype(jnp.int32) for r in ranges])

    def padded(tail):
        return jnp.pad(tail, ((HALO - tail.shape[0], 0), (0, 0)))

    x_conv, bc_conv, added = front(
        first,
        x_pre,
        bc_pre,
        padded(cut(tail_x, half, chans, 1)),
        padded(tail_bc),
        cut(conv_x, half, chans, 1),
        conv_bc,
        remaining,
    )

    inside = [jnp.zeros_like(added[:, 0])]
    for b in range(blocks):
        inside.append(block_decay[:, b] * inside[-1] + added[:, b])
    ending = inside.pop()

    group = 4
    across = swapped(ending.astype(BF16), "seq", 1).astype(F32)
    ended = {0: ending[0], PAIR: ending[1], 1: across[0], PAIR | 1: across[1]}
    base = (me // group) * group
    groups = seq_count // group
    total = 0.0
    for mask, value in ended.items():
        total = total + decay_between((me ^ mask) + 1, base + group) * value
    carry = shifted(total.astype(BF16), "seq", group).astype(F32)
    covered = 1
    while covered < groups - 1:
        more = shifted(carry.astype(BF16), "seq", group * covered).astype(F32)
        carry = carry + decay_between(base - group * covered, base) * more
        covered *= 2
    begin = cut(state_in, half, heads, 0).transpose(2, 0, 1).reshape(nstate, chans)
    incoming = []
    for place in ranges:
        value = decay_between(0, place) * begin + decay_between(base, place) * carry
        for mask, ended_value in ended.items():
            scale = jnp.where((me ^ mask) < place, decay_between((me ^ mask) + 1, place), 0.0)
            value = value + scale * ended_value
        incoming.append(value)
    opening = jnp.stack(incoming)
    states = []
    for b in range(blocks):
        states.append(opening + inside[b])
        opening = block_decay[:, b] * opening

    y_in = intra(x_conv, bc_conv, cum, cumt, heads)
    gated, squares = gate(
        y_in,
        x_conv,
        bc_conv,
        jnp.stack(states, axis=1),
        grown,
        jnp.repeat(cut(skip_gain, half, heads, 0), head_dim)[None, :],
        z_val,
        cut(norm_gain, half, chans, 0)[None, :],
    )

    per = seq_count // head_count
    relation = (me // per) ^ mine
    flat = gated.reshape(2 * rows, chans)

    def by_destination(low):
        return by_xor([out_pieces[q * per + low] for q in range(head_count)], relation)

    def send_far(weights):
        far = jnp.concatenate(weights[1::2], axis=1)
        return swapped(dot(flat, far).astype(BF16), "head", 1).astype(F32)

    def fold_head(parts):
        bit = 2
        while len(parts) > 1:
            sent = jnp.concatenate(parts[1::2], axis=1) if len(parts) > 2 else parts[1]
            got = swapped(sent.astype(BF16), "head", bit).astype(F32)
            parts = columns_added(parts[::2], got)
            bit *= 2
        return parts[0]

    def columns_added(parts, got):
        width = parts[0].shape[1]
        return [part + got[:, i * width : (i + 1) * width] for i, part in enumerate(parts)]

    def swap_pair(value):
        return swapped(value.astype(BF16), "seq", PAIR).astype(F32)

    done = {}
    lows = {low: by_destination(low) for low in range(per)}
    got_far = {low: send_far(lows[low]) for low in range(per)}
    for low in range(0, per, 2):
        parts = columns_added([dot(flat, w) for w in lows[low][::2]], got_far[low])
        whole = fold_head(parts)
        done[low] = whole[:rows] + swap_pair(whole[rows:])
    for low in range(1, per, 2):
        near = lows[low][::2]
        away = swap_pair(dot(gated[1], jnp.concatenate(near, axis=1)) + got_far[low][rows:])
        here = columns_added([dot(gated[0], w) for w in near], got_far[low][:rows])
        done[low] = fold_head(columns_added(here, away))

    squares = after(squares[:, :, 0], got_far[per - 1])
    squares = squares[0] + swapped(squares[1], "seq", PAIR)
    bit = 1
    while bit < head_count:
        squares = squares + swapped(squares, "head", bit)
        bit *= 2
    scale = lax.rsqrt(squares / inner + 1e-05)[:, None]
    result = by_xor([done[low] for low in range(per)], me % per)
    return jnp.concatenate([(piece * scale).astype(BF16) for piece in result], axis=1)


def solution(mesh):
    return jax.shard_map(
        local,
        mesh=mesh,
        in_specs=(
            P("seq", None),
            P("seq", None, "head"),
            P("seq", None),
            P(None, "head"),
            P(),
            P(None, "head"),
            P(),
            P("seq", "head"),
            P("head"),
            P("head", None, None),
            P("head"),
            P("head", "seq"),
        ),
        out_specs=P("seq", "head"),
        check_vma=False,
    )
```

```python
import functools

import jax
import jax.numpy as jnp
from jax import lax
from jax.experimental import pallas as pl
from jax.experimental.pallas import tpu as pltpu
from jax.sharding import PartitionSpec as P

Q = 256
HALO = 16
PAIR = 2
F32 = jnp.float32
BF16 = jnp.bfloat16
VMEM_LIMIT = 48 * 1024 * 1024
LIGHT = pl.CostEstimate(flops=1, bytes_accessed=1, transcendentals=0)


def swapped(value, axis, bit):
    size = lax.axis_size(axis)
    return lax.ppermute(value, axis, [(i, i ^ bit) for i in range(size)])


def shifted(value, axis, by):
    size = lax.axis_size(axis)
    return lax.ppermute(value, axis, [(i, i + by) for i in range(size - by)])


def cut(value, index, size, axis):
    return lax.dynamic_slice_in_dim(value, index * size, size, axis)


def after(value, *others):
    return lax.optimization_barrier((value, *others))[0]


ORDER = (
    ("x6 z4 x3 x5", "x1 x2 x4 z1"),
    ("t1 z2 w1 w4", "x3 x5 x6 t0"),
    ("x7 w2 z5", "z2 w1 z4"),
    ("t2 z6 z3 w5", "t1 x7 w2 z5 w4"),
    ("w6", "w4 w2"),
    ("z7", "z6 z3 w5 t2"),
    ("w3", "z7"),
)
WAITS = {send: waits.split() for sends, waits in ORDER for send in sends.split()}


class Sends:
    def __init__(self, own, given, quarter):
        self.own, self.given, self.quarter = own, given, quarter
        self.made = {}

    def get(self, kind, mask):
        name = f"{kind}{mask}"
        if name not in self.made:
            self.made[name] = self.tokens(mask) if kind == "t" else self.piece(kind, mask)
        return self.made[name]

    def waiting(self, kind, mask, value):
        others = [self.get(name[0], int(name[1:])) for name in WAITS.get(f"{kind}{mask}", ())]
        return after(value, *others) if others else value

    def piece(self, kind, mask):
        if mask == 0:
            return self.own[kind]
        if mask == PAIR:
            bit, value = PAIR, self.given[kind]
        else:
            bit = 1 if mask & 1 else 1 << (mask.bit_length() - 1)
            value = self.get(kind, mask ^ bit)
        return swapped(self.waiting(kind, mask, value), "seq", bit)

    def tokens(self, step):
        if step == 0:
            return swapped(self.waiting("t", 0, self.quarter), "seq", PAIR)
        if step == 1:
            value = self.get("t", 0)[None]
            bit = lax.axis_size("head") // 2
            while bit > 1:
                got = swapped(self.waiting("t", 1, value), "head", bit)
                value = jnp.concatenate([value, got])
                bit //= 2
            return value
        return swapped(self.waiting("t", 2, self.get("t", 1)), "head", 1)


def natural(value, axis_name, bit, axis):
    other = swapped(value, axis_name, bit)
    low = (lax.axis_index(axis_name) & bit) == 0
    return jnp.where(
        low, jnp.concatenate([value, other], axis=axis), jnp.concatenate([other, value], axis=axis)
    )


def by_xor(values, index):
    bit = 1
    while bit < len(values):
        flip = (index & bit) != 0
        values = [jnp.where(flip, values[j ^ bit], values[j]) for j in range(len(values))]
        bit *= 2
    return values


def dot(a, b):
    return jnp.dot(a, b, preferred_element_type=F32)


def front_kernel(
    first_ref, x_ref, bc_ref, tx_ref, tbc_ref, kx_ref, kbc_ref, dec_ref, xc_ref, bcc_ref, f_ref
):
    rows = xc_ref.shape[1]
    for r in range(2):
        is_first = first_ref[r] == 1

        def conv(pre_ref, tail_ref, k_ref):
            halo = jnp.where(is_first, tail_ref[...].astype(F32), pre_ref[r, :HALO].astype(F32))
            body = pre_ref[r, HALO:].astype(F32)
            whole = jnp.concatenate([halo, body], axis=0)
            taps = k_ref.shape[0]
            total = jnp.zeros(body.shape, F32)
            for k in range(taps):
                start = HALO - (taps - 1) + k
                total = total + k_ref[k : k + 1, :] * whole[start : start + rows]
            return (total * jax.nn.sigmoid(total)).astype(BF16)

        x_val = conv(x_ref, tx_ref, kx_ref)
        bc_val = conv(bc_ref, tbc_ref, kbc_ref)
        xc_ref[r] = x_val
        bcc_ref[r] = bc_val
        decayed = (x_val.astype(F32) * dec_ref[r]).astype(BF16)
        nstate = bc_val.shape[1] // 2
        for start in range(0, rows, Q):
            f_ref[r, start // Q] = lax.dot_general(
                bc_val[start : start + Q, :nstate],
                decayed[start : start + Q],
                (((0,), (0,)), ((), ())),
                preferred_element_type=F32,
            )


def intra_kernel(heads, x_ref, bc_ref, cum_ref, cumt_ref, y_ref):
    nstate = bc_ref.shape[2] // 2
    span = x_ref.shape[1]
    head_dim = x_ref.shape[2] // heads
    b_val = bc_ref[0, :, :nstate]
    c_val = bc_ref[0, :, nstate:]
    scores = lax.dot_general(c_val, b_val, (((1,), (1,)), ((), ())), preferred_element_type=F32)
    lower = lax.broadcasted_iota(jnp.int32, (span, span), 0) >= lax.broadcasted_iota(jnp.int32, (span, span), 1)
    scores = jnp.where(lower, scores, 0.0)
    pair = 128 // head_dim
    for start in range(0, heads, pair):
        outs = []
        for h in range(start, start + pair):
            diff = cum_ref[0, :, h : h + 1] - cumt_ref[0, 0, h : h + 1, :]
            weights = (jnp.exp(jnp.where(lower, diff, 0.0)) * scores).astype(BF16)
            outs.append(dot(weights, x_ref[0, :, h * head_dim : (h + 1) * head_dim]))
        y_ref[0, :, start * head_dim : (start + pair) * head_dim] = jnp.concatenate(outs, axis=1)


def gate_kernel(y_ref, x_ref, bc_ref, st_ref, e_ref, skip_ref, z_ref, gain_ref, g_ref, ss_ref):
    nstate = st_ref.shape[2]
    c_val = bc_ref[0, :, nstate:]
    state = st_ref[0, 0]
    high = state.astype(BF16)
    low = (state - high.astype(F32)).astype(BF16)
    carried = dot(c_val, high) + dot(c_val, low)
    y_val = (y_ref[0] + e_ref[0] * carried) / nstate + skip_ref[...] * x_ref[0].astype(F32)
    z_val = z_ref[0].astype(F32)
    gated = y_val * (z_val * jax.nn.sigmoid(z_val))
    g_ref[0] = (gated * gain_ref[...]).astype(BF16)
    total = jnp.sum(gated * gated, axis=1, keepdims=True)
    ss_ref[0] = jnp.broadcast_to(total, ss_ref.shape[1:])


def params(grid):
    return pltpu.CompilerParams(dimension_semantics=("arbitrary",) * grid, vmem_limit_bytes=VMEM_LIMIT)


def whole_block(shape):
    return pl.BlockSpec(shape, lambda *_: (0,) * len(shape))


def front(first, x_pre, bc_pre, tail_x, tail_bc, conv_x, conv_bc, decay):
    rows, chans = x_pre.shape[1] - HALO, x_pre.shape[2]
    bcw = bc_pre.shape[2]
    return pl.pallas_call(
        front_kernel,
        in_specs=[pl.BlockSpec(memory_space=pltpu.SMEM)] + [pl.BlockSpec(memory_space=pltpu.VMEM)] * 7,
        out_specs=[pl.BlockSpec(memory_space=pltpu.VMEM)] * 3,
        out_shape=[
            jax.ShapeDtypeStruct((2, rows, chans), BF16),
            jax.ShapeDtypeStruct((2, rows, bcw), BF16),
            jax.ShapeDtypeStruct((2, rows // Q, bcw // 2, chans), F32),
        ],
        compiler_params=pltpu.CompilerParams(vmem_limit_bytes=VMEM_LIMIT),
        cost_estimate=LIGHT,
        name="front",
    )(first, x_pre, bc_pre, tail_x, tail_bc, conv_x, conv_bc, decay)


def project_kernel(depth, with_halo, one_weight, place_ref, *refs):
    refs = list(refs)
    out_ref = refs.pop()
    halo_ref = refs.pop(0) if with_halo else None
    tokens_ref, others_ref = refs[:2]
    rows = tokens_ref.shape[0]
    lead = HALO if with_halo else 0
    totals = [None] * 3
    for k in range(place_ref.shape[1]):
        start = pl.multiple_of(place_ref[0, k], depth)
        place = pl.multiple_of(place_ref[2, k], depth)
        weight = refs[2][pl.ds(start, depth), :] if one_weight else refs[2 + k][:depth]
        lefts = [tokens_ref[:, pl.ds(start, depth)], others_ref[place_ref[1, k], :rows, pl.ds(place, depth)]]
        if with_halo:
            lefts.append(halo_ref[:, pl.ds(start, depth)])
        for i, left in enumerate(lefts):
            term = dot(left, weight)
            totals[i] = term if totals[i] is None else totals[i] + term
    for r in range(2):
        out_ref[r, lead:] = totals[r].astype(BF16)
        if with_halo:
            out_ref[r, :lead] = totals[2][r * HALO : (r + 1) * HALO].astype(BF16)


def project(places, depth, tokens, others, weights, halo=None):
    rows = tokens.shape[0] + (0 if halo is None else HALO)
    chans = weights[0].shape[1]
    operands = ([] if halo is None else [halo]) + [tokens, others] + list(weights)
    return pl.pallas_call(
        functools.partial(project_kernel, depth, halo is not None, len(weights) == 1),
        in_specs=[pl.BlockSpec(memory_space=pltpu.SMEM)]
        + [pl.BlockSpec(memory_space=pltpu.VMEM)] * len(operands),
        out_specs=pl.BlockSpec(memory_space=pltpu.VMEM),
        out_shape=jax.ShapeDtypeStruct((2, rows, chans), BF16),
        compiler_params=pltpu.CompilerParams(vmem_limit_bytes=VMEM_LIMIT),
        cost_estimate=LIGHT,
        name="project",
    )(places, *operands)


def intra(x_conv, bc_conv, cum, cumt, heads):
    _, rows, chans = x_conv.shape
    bcw = bc_conv.shape[2]
    blocks = rows // Q

    def tile(w):
        return pl.BlockSpec((1, Q, w), lambda r, i: (r, i, 0))

    return pl.pallas_call(
        functools.partial(intra_kernel, heads),
        grid=(2, blocks),
        in_specs=[tile(chans), tile(bcw), tile(heads), pl.BlockSpec((1, 1, heads, Q), lambda r, i: (r, i, 0, 0))],
        out_specs=tile(chans),
        out_shape=jax.ShapeDtypeStruct((2, rows, chans), F32),
        compiler_params=params(2),
        cost_estimate=LIGHT,
        name="intra",
    )(x_conv, bc_conv, cum, cumt)


def gate(y_in, x_conv, bc_conv, state, grown, skip, z_val, gain):
    _, rows, chans = x_conv.shape
    bcw = bc_conv.shape[2]

    def tile(w):
        return pl.BlockSpec((1, Q, w), lambda r, i: (r, i, 0))

    return pl.pallas_call(
        gate_kernel,
        grid=(2, rows // Q),
        in_specs=[
            tile(chans),
            tile(chans),
            tile(bcw),
            pl.BlockSpec((1, 1, bcw // 2, chans), lambda r, i: (r, i, 0, 0)),
            tile(chans),
            whole_block((1, chans)),
            tile(chans),
            whole_block((1, chans)),
        ],
        out_specs=[tile(chans), tile(128)],
        out_shape=[
            jax.ShapeDtypeStruct((2, rows, chans), BF16),
            jax.ShapeDtypeStruct((2, rows, 128), F32),
        ],
        compiler_params=params(2),
        cost_estimate=LIGHT,
        name="gate",
    )(y_in, x_conv, bc_conv, state, grown, skip, z_val, gain)


def local(
    tokens,
    w_xz,
    w_bc,
    conv_x,
    conv_bc,
    tail_x,
    tail_bc,
    decay_code,
    skip_gain,
    state_in,
    norm_gain,
    w_out,
):
    rows = tokens.shape[0]
    all_heads, head_dim, nstate = state_in.shape
    seq_count = lax.axis_size("seq")
    head_count = lax.axis_size("head")
    inner = all_heads * head_dim * head_count
    me = lax.axis_index("seq")
    mine = lax.axis_index("head")
    half = (me // PAIR) % 2
    heads = all_heads // 2
    chans = heads * head_dim
    depth = w_xz.shape[0]

    lag = conv_x.shape[0] - 1
    code_sums = jnp.sum(decay_code, axis=0)
    digits = jnp.stack([(code_sums >> (8 * j)) & 255 for j in range(4)]).reshape(1, -1).astype(BF16)
    last_rows = tokens[rows - lag :].reshape(-1, chans)
    halo_rows = last_rows.shape[0]
    spare = -(halo_rows + 1) % 16
    extra = jnp.concatenate(
        [last_rows, jnp.pad(digits, ((0, spare), (0, chans - digits.shape[1])))], axis=0
    )

    share = tokens.shape[1] // head_count
    codes = decay_code.T
    given = cut(codes, 1 - half, heads, 0)
    given = jnp.stack([(given >> (8 * j)) & 255 for j in range(3)]).reshape(-1, share).astype(BF16)
    code_rows = given.shape[0]
    given = jnp.pad(given, ((0, -code_rows % 16), (0, 0)))

    flat_w = lax.optimization_barrier(w_xz.reshape(depth, -1))
    full = flat_w.shape[1] // 2
    x_w, z_w = flat_w[:, :full], flat_w[:, full:]
    own = {
        "x": jnp.concatenate([cut(x_w, half, chans, 1), extra]),
        "z": cut(z_w, half, chans, 1),
        "w": cut(w_out, half, chans, 0),
    }
    other_half = {
        "x": jnp.concatenate([cut(x_w, 1 - half, chans, 1), extra]),
        "z": cut(z_w, 1 - half, chans, 1),
        "w": cut(w_out, 1 - half, chans, 0),
    }
    sends = Sends(own, other_half, jnp.concatenate([cut(tokens, mine, share, 1), given]))
    masks = list(range(seq_count))
    x_pieces, z_pieces, out_pieces = [{mask: sends.get(kind, mask) for mask in masks} for kind in "xzw"]

    others = jnp.concatenate([sends.get("t", 1), sends.get("t", 2)])
    ranges = [me, me ^ PAIR]
    extras = jnp.stack([x_pieces[mask][depth:] for mask in range(seq_count)])

    def rows_before(place):
        got = lax.dynamic_index_in_dim(extras, (me ^ (place - 1)) & (seq_count - 1), 0, keepdims=False)
        return jnp.pad(got[:halo_rows].reshape(lag, -1), ((HALO - lag, 0), (0, 0)))

    halo = jnp.concatenate([rows_before(place) for place in ranges], axis=0)

    starts = [(me ^ mask) * depth for mask in masks]
    blocks = [a // share ^ mine for a in starts]
    blocks = [(b >> 1) + (b & 1) * (head_count // 2) for b in blocks]
    spots = [starts, blocks, [a % share for a in starts]]
    spots = jnp.stack([jnp.stack([jnp.int32(a) for a in row]) for row in spots])

    part = depth // head_count
    w_bc_all = lax.all_gather(cut(w_bc, mine, part, 0), ("seq", "head"), axis=0, tiled=True)
    bc_pre = project(spots, depth, tokens, others, [w_bc_all], halo)
    x_pre = project(spots, depth, tokens, others, list(x_pieces.values()), halo)
    z_val = project(spots, depth, tokens, others, list(z_pieces.values()))

    per_code = -1.0 / (16.0 * rows * seq_count)
    got = sends.get("t", 0)[rows : rows + code_rows].astype(F32).reshape(3, heads, rows)
    other_codes = got[0] + 256.0 * got[1] + 65536.0 * got[2]
    ld = jnp.stack([cut(codes, half, heads, 0).astype(F32), other_codes]) * per_code
    blocks = rows // Q
    cumt = jnp.cumsum(ld.reshape(2, heads, blocks, Q), axis=3).transpose(0, 2, 1, 3)
    cum = cumt.transpose(0, 1, 3, 2)
    ends = cum[:, :, -1:, :]
    remaining = jnp.repeat(jnp.exp(ends - cum).reshape(2, rows, heads), head_dim, axis=2)
    block_decay = jnp.repeat(jnp.exp(ends), head_dim, axis=3)
    cum = cum.reshape(2, rows, heads)
    grown = jnp.repeat(jnp.exp(cum), head_dim, axis=2)
    totals = jnp.stack([x_pieces[mask][depth + halo_rows] for mask in masks])
    totals = totals[:, : 4 * all_heads].astype(F32).reshape(-1, 4, all_heads)
    totals = sum(totals[:, j] * 256.0**j for j in range(4)) * per_code
    totals = cut(totals, half, heads, 1)
    places = me ^ jnp.array(masks, jnp.int32)

    def decay_between(low, high):
        chosen = jnp.where((places >= low) & (places < high), 1.0, 0.0)[:, None]
        return jnp.repeat(jnp.exp(jnp.sum(chosen * totals, axis=0)), head_dim)[None, :]

    first = jnp.stack([(r == 0).astype(jnp.int32) for r in ranges])

    def padded(tail):
        return jnp.pad(tail, ((HALO - tail.shape[0], 0), (0, 0)))

    x_conv, bc_conv, added = front(
        after(first, sends.get("w", PAIR)),
        x_pre,
        bc_pre,
        padded(cut(tail_x, half, chans, 1)),
        padded(tail_bc),
        cut(conv_x, half, chans, 1),
        conv_bc,
        remaining,
    )

    inside = [jnp.zeros_like(added[:, 0])]
    for b in range(blocks):
        inside.append(block_decay[:, b] * inside[-1] + added[:, b])
    ending = inside.pop()

    group = 4
    across = swapped(ending.astype(BF16), "seq", 1).astype(F32)
    ended = {0: ending[0], PAIR: ending[1], 1: across[0], PAIR | 1: across[1]}
    base = (me // group) * group
    groups = seq_count // group
    total = 0.0
    for mask, value in ended.items():
        total = total + decay_between((me ^ mask) + 1, base + group) * value
    carry = shifted(total.astype(BF16), "seq", group).astype(F32)
    covered = 1
    while covered < groups - 1:
        more = shifted(carry.astype(BF16), "seq", group * covered).astype(F32)
        carry = carry + decay_between(base - group * covered, base) * more
        covered *= 2
    begin = cut(state_in, half, heads, 0).transpose(2, 0, 1).reshape(nstate, chans)
    incoming = []
    for place in ranges:
        value = decay_between(0, place) * begin + decay_between(base, place) * carry
        for mask, ended_value in ended.items():
            scale = jnp.where((me ^ mask) < place, decay_between((me ^ mask) + 1, place), 0.0)
            value = value + scale * ended_value
        incoming.append(value)
    opening = jnp.stack(incoming)
    states = []
    for b in range(blocks):
        states.append(opening + inside[b])
        opening = block_decay[:, b] * opening

    y_in = intra(x_conv, bc_conv, cum, cumt, heads)
    gated, squares = gate(
        y_in,
        x_conv,
        bc_conv,
        jnp.stack(states, axis=1),
        grown,
        jnp.repeat(cut(skip_gain, half, heads, 0), head_dim)[None, :],
        z_val,
        after(cut(norm_gain, half, chans, 0)[None, :], out_pieces[PAIR | 1]),
    )

    per = seq_count // head_count
    relation = (me // per) ^ mine
    flat = gated.reshape(2 * rows, chans)

    def by_destination(low):
        return by_xor([out_pieces[q * per + low] for q in range(head_count)], relation)

    def send_far(weights):
        far = jnp.concatenate(weights[1::2], axis=1)
        return swapped(dot(flat, far).astype(BF16), "head", 1).astype(F32)

    def fold_head(parts):
        bit = 2
        while len(parts) > 1:
            sent = jnp.concatenate(parts[1::2], axis=1) if len(parts) > 2 else parts[1]
            got = swapped(sent.astype(BF16), "head", bit).astype(F32)
            parts = columns_added(parts[::2], got)
            bit *= 2
        return parts[0]

    def columns_added(parts, got):
        width = parts[0].shape[1]
        return [part + got[:, i * width : (i + 1) * width] for i, part in enumerate(parts)]

    def swap_pair(value):
        return swapped(value.astype(BF16), "seq", PAIR).astype(F32)

    squares = squares[0, :, 0] + swapped(squares[1, :, 0], "seq", PAIR)
    paired = squares
    bit = head_count // 2
    while bit >= 1:
        upper = squares
        squares = squares + swapped(squares, "head", bit)
        bit //= 2
    scale = lax.rsqrt(squares / inner + 1e-05)[:, None]

    done = {}
    for low in range(0, per, 2):
        weights = by_destination(low)
        got_far = send_far(weights)
        parts = columns_added([dot(flat, w) for w in weights[::2]], got_far)
        parts = [after(part, upper) if i else part for i, part in enumerate(parts)]
        whole = fold_head(parts)
        done[low] = whole[:rows] + swap_pair(whole[rows:])
    flat = after(flat, paired)
    for low in range(1, per, 2):
        weights = by_destination(low)
        got_far = send_far(weights)
        near = weights[::2]
        away = swap_pair(dot(gated[1], jnp.concatenate(near, axis=1)) + got_far[rows:])
        here = columns_added([dot(gated[0], w) for w in near], got_far[:rows])
        done[low] = fold_head(columns_added(here, away))

    result = by_xor([done[low] for low in range(per)], me % per)
    return jnp.concatenate([(piece * scale).astype(BF16) for piece in result], axis=1)


def solution(mesh):
    return jax.shard_map(
        local,
        mesh=mesh,
        in_specs=(
            P("seq", None),
            P("seq", None, "head"),
            P("seq", None),
            P(None, "head"),
            P(),
            P(None, "head"),
            P(),
            P("seq", "head"),
            P("head"),
            P("head", None, None),
            P("head"),
            P("head", "seq"),
        ),
        out_specs=P("seq", "head"),
        check_vma=False,
    )
```

```python
import functools

import jax
import jax.numpy as jnp
from jax import lax
from jax.experimental import pallas as pl
from jax.experimental.pallas import tpu as pltpu
from jax.sharding import PartitionSpec as P

Q = 256
HALO = 16
PAIR = 2
F32 = jnp.float32
BF16 = jnp.bfloat16
VMEM_LIMIT = 48 * 1024 * 1024
LIGHT = pl.CostEstimate(flops=1, bytes_accessed=1, transcendentals=0)


def swapped(value, axis, bit):
    size = lax.axis_size(axis)
    return lax.ppermute(value, axis, [(i, i ^ bit) for i in range(size)])


def shifted(value, axis, by):
    size = lax.axis_size(axis)
    return lax.ppermute(value, axis, [(i, i + by) for i in range(size - by)])


def cut(value, index, size, axis):
    return lax.dynamic_slice_in_dim(value, index * size, size, axis)


def after(value, *others):
    return lax.optimization_barrier((value, *others))[0]


ORDER = (
    ("front", "t2"),
    ("t1", "t0 x3 x5 x6"),
    ("t2", "t1 w2 w4 x7 z5"),
    ("w1", "t0 x3 x5 x6"),
    ("w2", "w1 z2 z4"),
    ("w3", "z7"),
    ("w4", "t0 x3 x5 x6"),
    ("w5", "t1 w2 w4 x7 z5"),
    ("w6", "w2 w4"),
    ("x3", "x2 x4 z1"),
    ("x5", "x1 x2 x4 z1"),
    ("x6", "x1 x2 x4 z1"),
    ("x7", "w1 z2 z4"),
    ("z2", "t0 x3 x5 x6"),
    ("z3", "t1 w2 w4 x7 z5"),
    ("z4", "x1 x2 x4 z1"),
    ("z5", "w1 z4"),
    ("z6", "t1 w2 w4 x7 z5"),
    ("z7", "t2 w5 z3 z6"),
)
WAITS = {send: waits.split() for sends, waits in ORDER for send in sends.split()}


class Sends:
    def __init__(self, own, given, quarter):
        self.own, self.given, self.quarter = own, given, quarter
        self.made = {}

    def get(self, kind, mask):
        name = f"{kind}{mask}"
        if name not in self.made:
            self.made[name] = self.tokens(mask) if kind == "t" else self.piece(kind, mask)
        return self.made[name]

    def held(self, name, value):
        others = [self.get(other[0], int(other[1:])) for other in WAITS.get(name, ())]
        return after(value, *others) if others else value

    def waiting(self, kind, mask, value):
        return self.held(f"{kind}{mask}", value)

    def piece(self, kind, mask):
        if mask == 0:
            return self.own[kind]
        if mask == PAIR:
            bit, value = PAIR, self.given[kind]
        else:
            bit = 1 if mask & 1 else 1 << (mask.bit_length() - 1)
            value = self.get(kind, mask ^ bit)
        return swapped(self.waiting(kind, mask, value), "seq", bit)

    def tokens(self, step):
        if step == 0:
            return swapped(self.waiting("t", 0, self.quarter), "seq", PAIR)
        if step == 1:
            value = self.get("t", 0)[None]
            bit = lax.axis_size("head") // 2
            while bit > 1:
                got = swapped(self.waiting("t", 1, value), "head", bit)
                value = jnp.concatenate([value, got])
                bit //= 2
            return value
        return swapped(self.waiting("t", 2, self.get("t", 1)), "head", 1)


def by_xor(values, index):
    bit = 1
    while bit < len(values):
        flip = (index & bit) != 0
        values = [jnp.where(flip, values[j ^ bit], values[j]) for j in range(len(values))]
        bit *= 2
    return values


def dot(a, b):
    return jnp.dot(a, b, preferred_element_type=F32)


def by_lanes(value, head_dim):
    heads = value.shape[1]
    pair = 128 // head_dim
    lane = lax.broadcasted_iota(jnp.int32, (value.shape[0], 128), 1) // head_dim
    wide = []
    for start in range(0, heads, pair):
        part = jnp.broadcast_to(value[:, start : start + 1], lane.shape)
        for h in range(1, pair):
            part = jnp.where(lane == h, value[:, start + h : start + h + 1], part)
        wide.append(part)
    return jnp.concatenate(wide, axis=1)


def slice_of_others(even_ref, odd_ref, place_ref, k, rows, depth):
    columns = pl.ds(pl.multiple_of(place_ref[2, k], depth), depth)
    block = place_ref[1, k]
    return jnp.where(place_ref[3, k] == 1, odd_ref[block, rows, columns], even_ref[block, rows, columns])


def front_kernel(
    first_ref, x_ref, bc_ref, tx_ref, tbc_ref, kx_ref, kbc_ref, cum_ref, xc_ref, bcc_ref, f_ref
):
    rows = xc_ref.shape[1]
    for r in range(2):
        is_first = first_ref[r] == 1

        def conv(pre_ref, tail_ref, k_ref):
            halo = jnp.where(is_first, tail_ref[...].astype(F32), pre_ref[r, :HALO].astype(F32))
            body = pre_ref[r, HALO:].astype(F32)
            whole = jnp.concatenate([halo, body], axis=0)
            taps = k_ref.shape[0]
            total = jnp.zeros(body.shape, F32)
            for k in range(taps):
                start = HALO - (taps - 1) + k
                total = total + k_ref[k : k + 1, :] * whole[start : start + rows]
            return (total * jax.nn.sigmoid(total)).astype(BF16)

        x_val = conv(x_ref, tx_ref, kx_ref)
        bc_val = conv(bc_ref, tbc_ref, kbc_ref)
        xc_ref[r] = x_val
        bcc_ref[r] = bc_val
        nstate = bc_val.shape[1] // 2
        head_dim = x_val.shape[1] // cum_ref.shape[2]
        for start in range(0, rows, Q):
            cum = cum_ref[r, start : start + Q]
            remaining = by_lanes(jnp.exp(cum[Q - 1 :] - cum), head_dim)
            decayed = (x_val[start : start + Q].astype(F32) * remaining).astype(BF16)
            f_ref[r, start // Q] = lax.dot_general(
                bc_val[start : start + Q, :nstate],
                decayed,
                (((0,), (0,)), ((), ())),
                preferred_element_type=F32,
            )


def intra_kernel(heads, x_ref, bc_ref, cum_ref, cumt_ref, y_ref):
    nstate = bc_ref.shape[2] // 2
    span = x_ref.shape[1]
    head_dim = x_ref.shape[2] // heads
    b_val = bc_ref[0, :, :nstate]
    c_val = bc_ref[0, :, nstate:]
    scores = lax.dot_general(c_val, b_val, (((1,), (1,)), ((), ())), preferred_element_type=F32)
    lower = lax.broadcasted_iota(jnp.int32, (span, span), 0) >= lax.broadcasted_iota(jnp.int32, (span, span), 1)
    scores = jnp.where(lower, scores, 0.0)
    pair = 128 // head_dim
    for start in range(0, heads, pair):
        outs = []
        for h in range(start, start + pair):
            diff = cum_ref[0, :, h : h + 1] - cumt_ref[0, 0, h : h + 1, :]
            weights = (jnp.exp(jnp.where(lower, diff, 0.0)) * scores).astype(BF16)
            outs.append(dot(weights, x_ref[0, :, h * head_dim : (h + 1) * head_dim]))
        y_ref[0, :, start * head_dim : (start + pair) * head_dim] = jnp.concatenate(outs, axis=1)


def gate_kernel(
    place_ref, y_ref, x_ref, bc_ref, st_ref, cum_ref, skip_ref, z_ref, gain_ref, tokens_ref, even_ref, odd_ref,
    w_ref, g_ref, ss_ref
):
    nstate = st_ref.shape[2]
    depth = w_ref.shape[0]
    rows = pl.ds(pl.multiple_of(pl.program_id(1) * Q, Q), Q)
    own = tokens_ref[rows, pl.ds(pl.multiple_of(place_ref[0, 0], depth), depth)]
    other = slice_of_others(even_ref, odd_ref, place_ref, 0, rows, depth)
    left = jnp.where(pl.program_id(0) == 0, own, other)
    z_val = (z_ref[0] + dot(left, w_ref[...])).astype(BF16).astype(F32)
    c_val = bc_ref[0, :, nstate:]
    state = st_ref[0, 0]
    high = state.astype(BF16)
    low = (state - high.astype(F32)).astype(BF16)
    carried = dot(c_val, high) + dot(c_val, low)
    grown = by_lanes(jnp.exp(cum_ref[0]), x_ref.shape[2] // cum_ref.shape[2])
    y_val = (y_ref[0] + grown * carried) / nstate + skip_ref[...] * x_ref[0].astype(F32)
    gated = y_val * (z_val * jax.nn.sigmoid(z_val))
    g_ref[0] = (gated * gain_ref[...]).astype(BF16)
    total = jnp.sum(gated * gated, axis=1, keepdims=True)
    ss_ref[0] = jnp.broadcast_to(total, ss_ref.shape[1:])


def params(grid):
    return pltpu.CompilerParams(dimension_semantics=("arbitrary",) * grid, vmem_limit_bytes=VMEM_LIMIT)


def whole_block(shape):
    return pl.BlockSpec(shape, lambda *_: (0,) * len(shape))


def front(first, x_pre, bc_pre, tail_x, tail_bc, conv_x, conv_bc, cum):
    rows, chans = x_pre.shape[1] - HALO, x_pre.shape[2]
    bcw = bc_pre.shape[2]
    return pl.pallas_call(
        front_kernel,
        in_specs=[pl.BlockSpec(memory_space=pltpu.SMEM)] + [pl.BlockSpec(memory_space=pltpu.VMEM)] * 7,
        out_specs=[pl.BlockSpec(memory_space=pltpu.VMEM)] * 3,
        out_shape=[
            jax.ShapeDtypeStruct((2, rows, chans), BF16),
            jax.ShapeDtypeStruct((2, rows, bcw), BF16),
            jax.ShapeDtypeStruct((2, rows // Q, bcw // 2, chans), F32),
        ],
        compiler_params=pltpu.CompilerParams(vmem_limit_bytes=VMEM_LIMIT),
        cost_estimate=LIGHT,
        name="front",
    )(first, x_pre, bc_pre, tail_x, tail_bc, conv_x, conv_bc, cum)


def project_kernel(depth, with_halo, one_weight, place_ref, *refs):
    refs = list(refs)
    out_ref = refs.pop()
    halo_ref = refs.pop(0) if with_halo else None
    tokens_ref, even_ref, odd_ref = refs[:3]
    rows = tokens_ref.shape[0]
    lead = HALO if with_halo else 0
    totals = [None] * 3
    for k in range(place_ref.shape[1]):
        start = pl.multiple_of(place_ref[0, k], depth)
        weight = refs[3][pl.ds(start, depth), :] if one_weight else refs[3 + k][:depth]
        lefts = [
            tokens_ref[:, pl.ds(start, depth)],
            slice_of_others(even_ref, odd_ref, place_ref, k, pl.ds(0, rows), depth),
        ]
        if with_halo:
            lefts.append(halo_ref[:, pl.ds(start, depth)])
        for i, left in enumerate(lefts):
            term = dot(left, weight)
            totals[i] = term if totals[i] is None else totals[i] + term
    for r in range(2):
        out_ref[r, lead:] = totals[r].astype(out_ref.dtype)
        if with_halo:
            out_ref[r, :lead] = totals[2][r * HALO : (r + 1) * HALO].astype(BF16)


def project(places, depth, tokens, others, weights, halo=None, dtype=BF16):
    rows = tokens.shape[0] + (0 if halo is None else HALO)
    chans = weights[0].shape[1]
    operands = ([] if halo is None else [halo]) + [tokens, *others] + list(weights)
    return pl.pallas_call(
        functools.partial(project_kernel, depth, halo is not None, len(weights) == 1),
        in_specs=[pl.BlockSpec(memory_space=pltpu.SMEM)]
        + [pl.BlockSpec(memory_space=pltpu.VMEM)] * len(operands),
        out_specs=pl.BlockSpec(memory_space=pltpu.VMEM),
        out_shape=jax.ShapeDtypeStruct((2, rows, chans), dtype),
        compiler_params=pltpu.CompilerParams(vmem_limit_bytes=VMEM_LIMIT),
        cost_estimate=LIGHT,
        name="project",
    )(places, *operands)


def intra(x_conv, bc_conv, cum, cumt, heads):
    _, rows, chans = x_conv.shape
    bcw = bc_conv.shape[2]
    blocks = rows // Q

    def tile(w):
        return pl.BlockSpec((1, Q, w), lambda r, i: (r, i, 0))

    return pl.pallas_call(
        functools.partial(intra_kernel, heads),
        grid=(2, blocks),
        in_specs=[tile(chans), tile(bcw), tile(heads), pl.BlockSpec((1, 1, heads, Q), lambda r, i: (r, i, 0, 0))],
        out_specs=tile(chans),
        out_shape=jax.ShapeDtypeStruct((2, rows, chans), F32),
        compiler_params=params(2),
        cost_estimate=LIGHT,
        name="intra",
    )(x_conv, bc_conv, cum, cumt)


def gate(places, y_in, x_conv, bc_conv, state, cum, skip, z_part, gain, tokens, others, z_weight):
    _, rows, chans = x_conv.shape
    bcw = bc_conv.shape[2]

    def tile(w):
        return pl.BlockSpec((1, Q, w), lambda r, i: (r, i, 0))

    return pl.pallas_call(
        gate_kernel,
        grid=(2, rows // Q),
        in_specs=[
            pl.BlockSpec(memory_space=pltpu.SMEM),
            tile(chans),
            tile(chans),
            tile(bcw),
            pl.BlockSpec((1, 1, bcw // 2, chans), lambda r, i: (r, i, 0, 0)),
            tile(cum.shape[2]),
            whole_block((1, chans)),
            tile(chans),
            whole_block((1, chans)),
        ]
        + [pl.BlockSpec(memory_space=pltpu.VMEM)] * 4,
        out_specs=[tile(chans), tile(128)],
        out_shape=[
            jax.ShapeDtypeStruct((2, rows, chans), BF16),
            jax.ShapeDtypeStruct((2, rows, 128), F32),
        ],
        compiler_params=params(2),
        cost_estimate=LIGHT,
        name="gate",
    )(places, y_in, x_conv, bc_conv, state, cum, skip, z_part, gain, tokens, *others, z_weight)


def local(
    tokens,
    w_xz,
    w_bc,
    conv_x,
    conv_bc,
    tail_x,
    tail_bc,
    decay_code,
    skip_gain,
    state_in,
    norm_gain,
    w_out,
):
    rows = tokens.shape[0]
    all_heads, head_dim, nstate = state_in.shape
    seq_count = lax.axis_size("seq")
    head_count = lax.axis_size("head")
    inner = all_heads * head_dim * head_count
    me = lax.axis_index("seq")
    mine = lax.axis_index("head")
    half = (me // PAIR) % 2
    heads = all_heads // 2
    chans = heads * head_dim
    depth = w_xz.shape[0]

    lag = conv_x.shape[0] - 1
    code_sums = jnp.sum(decay_code, axis=0)
    digits = jnp.stack([(code_sums >> (8 * j)) & 255 for j in range(4)]).reshape(1, -1).astype(BF16)
    last_rows = tokens[rows - lag :].reshape(-1, chans)
    halo_rows = last_rows.shape[0]
    spare = -(halo_rows + 1) % 16
    extra = jnp.concatenate(
        [last_rows, jnp.pad(digits, ((0, spare), (0, chans - digits.shape[1])))], axis=0
    )

    share = tokens.shape[1] // head_count
    codes = decay_code.T
    given = cut(codes, 1 - half, heads, 0)
    given = jnp.stack([(given >> (8 * j)) & 255 for j in range(3)]).reshape(-1, share).astype(BF16)
    code_rows = given.shape[0]
    given = jnp.pad(given, ((0, -code_rows % 16), (0, 0)))

    flat_w = lax.optimization_barrier(w_xz.reshape(depth, -1))
    full = flat_w.shape[1] // 2
    x_w, z_w = flat_w[:, :full], flat_w[:, full:]
    own = {
        "x": jnp.concatenate([cut(x_w, half, chans, 1), extra]),
        "z": cut(z_w, half, chans, 1),
        "w": cut(w_out, half, chans, 0),
    }
    other_half = {
        "x": jnp.concatenate([cut(x_w, 1 - half, chans, 1), extra]),
        "z": cut(z_w, 1 - half, chans, 1),
        "w": cut(w_out, 1 - half, chans, 0),
    }
    sends = Sends(own, other_half, jnp.concatenate([cut(tokens, mine, share, 1), given]))
    masks = list(range(seq_count))
    x_pieces, z_pieces, out_pieces = [{mask: sends.get(kind, mask) for mask in masks} for kind in "xzw"]

    others = (sends.get("t", 1), sends.get("t", 2))
    ranges = [me, me ^ PAIR]
    extras = [x_pieces[mask][depth:] for mask in range(seq_count)]

    def rows_before(place):
        got = by_xor([extra[:halo_rows] for extra in extras], (me ^ (place - 1)) & (seq_count - 1))[0]
        return jnp.pad(got.reshape(lag, -1), ((HALO - lag, 0), (0, 0)))

    halo = jnp.concatenate([rows_before(place) for place in ranges], axis=0)

    starts = [(me ^ mask) * depth for mask in masks]
    blocks = [a // share ^ mine for a in starts]
    spots = [starts, [b >> 1 for b in blocks], [a % share for a in starts], [b & 1 for b in blocks]]
    spots = jnp.stack([jnp.stack([jnp.int32(a) for a in row]) for row in spots])

    part = depth // head_count
    w_bc_all = lax.all_gather(cut(w_bc, mine, part, 0), ("seq", "head"), axis=0, tiled=True)
    bc_pre = project(sends.held("project_x", spots), depth, tokens, others, [w_bc_all], halo)
    x_pre = project(sends.held("project_x", spots), depth, tokens, others, list(x_pieces.values()), halo)
    z_part = project(
        sends.held("project_z", spots[:, :-1]), depth, tokens, others, list(z_pieces.values())[:-1], dtype=F32
    )

    per_code = -1.0 / (16.0 * rows * seq_count)
    got = sends.held("decays", sends.get("t", 0))[rows : rows + code_rows].astype(F32).reshape(3, heads, rows)
    other_codes = got[0] + 256.0 * got[1] + 65536.0 * got[2]
    ld = jnp.stack([cut(codes, half, heads, 0).astype(F32), other_codes]) * per_code
    blocks = rows // Q
    cumt = jnp.cumsum(ld.reshape(2, heads, blocks, Q), axis=3).transpose(0, 2, 1, 3)
    cum = cumt.transpose(0, 1, 3, 2)
    ends = cum[:, :, -1:, :]
    block_decay = jnp.repeat(jnp.exp(ends), head_dim, axis=3)
    cum = cum.reshape(2, rows, heads)
    totals = jnp.stack([x_pieces[mask][depth + halo_rows] for mask in masks])
    totals = totals[:, : 4 * all_heads].astype(F32).reshape(-1, 4, all_heads)
    totals = sum(totals[:, j] * 256.0**j for j in range(4)) * per_code
    totals = cut(totals, half, heads, 1)
    places = me ^ jnp.array(masks, jnp.int32)

    def decay_between(low, high):
        chosen = jnp.where((places >= low) & (places < high), 1.0, 0.0)[:, None]
        return jnp.repeat(jnp.exp(jnp.sum(chosen * totals, axis=0)), head_dim)[None, :]

    first = jnp.stack([(r == 0).astype(jnp.int32) for r in ranges])

    def padded(tail):
        return jnp.pad(tail, ((HALO - tail.shape[0], 0), (0, 0)))

    x_conv, bc_conv, added = front(
        sends.held("front", first),
        x_pre,
        bc_pre,
        padded(cut(tail_x, half, chans, 1)),
        padded(tail_bc),
        cut(conv_x, half, chans, 1),
        conv_bc,
        cum,
    )

    inside = [jnp.zeros_like(added[:, 0])]
    for b in range(blocks):
        inside.append(block_decay[:, b] * inside[-1] + added[:, b])
    ending = inside.pop()

    group = 4
    across = swapped(ending.astype(BF16), "seq", 1).astype(F32)
    ended = {0: ending[0], PAIR: ending[1], 1: across[0], PAIR | 1: across[1]}
    base = (me // group) * group
    groups = seq_count // group
    total = 0.0
    for mask, value in ended.items():
        total = total + decay_between((me ^ mask) + 1, base + group) * value
    carry = shifted(total.astype(BF16), "seq", group).astype(F32)
    covered = 1
    while covered < groups - 1:
        more = shifted(carry.astype(BF16), "seq", group * covered).astype(F32)
        carry = carry + decay_between(base - group * covered, base) * more
        covered *= 2
    begin = cut(state_in, half, heads, 0).transpose(2, 0, 1).reshape(nstate, chans)
    incoming = []
    for place in ranges:
        value = decay_between(0, place) * begin + decay_between(base, place) * carry
        for mask, ended_value in ended.items():
            scale = jnp.where((me ^ mask) < place, decay_between((me ^ mask) + 1, place), 0.0)
            value = value + scale * ended_value
        incoming.append(value)
    opening = jnp.stack(incoming)
    states = []
    for b in range(blocks):
        states.append(opening + inside[b])
        opening = block_decay[:, b] * opening

    y_in = intra(x_conv, bc_conv, cum, cumt, heads)
    gated, squares = gate(
        spots[:, -1:],
        y_in,
        x_conv,
        bc_conv,
        jnp.stack(states, axis=1),
        cum,
        jnp.repeat(cut(skip_gain, half, heads, 0), head_dim)[None, :],
        z_part,
        sends.held("gate", cut(norm_gain, half, chans, 0)[None, :]),
        tokens,
        others,
        z_pieces[masks[-1]],
    )

    per = seq_count // head_count
    relation = (me // per) ^ mine
    flat = gated.reshape(2 * rows, chans)

    def by_destination(low):
        return by_xor([out_pieces[q * per + low] for q in range(head_count)], relation)

    def send_far(weights):
        far = jnp.concatenate(weights[1::2], axis=1)
        return swapped(dot(flat, far).astype(BF16), "head", 1).astype(F32)

    def fold_head(parts):
        bit = 2
        while len(parts) > 1:
            sent = jnp.concatenate(parts[1::2], axis=1) if len(parts) > 2 else parts[1]
            got = swapped(sent.astype(BF16), "head", bit).astype(F32)
            parts = columns_added(parts[::2], got)
            bit *= 2
        return parts[0]

    def columns_added(parts, got):
        width = parts[0].shape[1]
        return [part + got[:, i * width : (i + 1) * width] for i, part in enumerate(parts)]

    def swap_pair(value):
        return swapped(value.astype(BF16), "seq", PAIR).astype(F32)

    squares = squares[0, :, 0] + swapped(squares[1, :, 0], "seq", PAIR)
    paired = squares
    bit = head_count // 2
    while bit >= 1:
        upper = squares
        squares = squares + swapped(squares, "head", bit)
        bit //= 2
    scale = lax.rsqrt(squares / inner + 1e-05)[:, None]

    done = {}
    for low in range(0, per, 2):
        weights = by_destination(low)
        got_far = send_far(weights)
        parts = columns_added([dot(flat, w) for w in weights[::2]], got_far)
        parts = [after(part, upper) if i else part for i, part in enumerate(parts)]
        whole = fold_head(parts)
        done[low] = whole[:rows] + swap_pair(whole[rows:])
    flat = after(flat, paired)
    for low in range(1, per, 2):
        weights = by_destination(low)
        got_far = send_far(weights)
        near = weights[::2]
        away = swap_pair(dot(gated[1], jnp.concatenate(near, axis=1)) + got_far[rows:])
        here = columns_added([dot(gated[0], w) for w in near], got_far[:rows])
        done[low] = fold_head(columns_added(here, away))

    result = by_xor([done[low] for low in range(per)], me % per)
    return jnp.concatenate([(piece * scale).astype(BF16) for piece in result], axis=1)


def solution(mesh):
    return jax.shard_map(
        local,
        mesh=mesh,
        in_specs=(
            P("seq", None),
            P("seq", None, "head"),
            P("seq", None),
            P(None, "head"),
            P(),
            P(None, "head"),
            P(),
            P("seq", "head"),
            P("head"),
            P("head", None, None),
            P("head"),
            P("head", "seq"),
        ),
        out_specs=P("seq", "head"),
        check_vma=False,
    )
```

```python
import functools

import jax
import jax.numpy as jnp
from jax import lax
from jax.experimental import pallas as pl
from jax.experimental.pallas import tpu as pltpu
from jax.sharding import PartitionSpec as P

Q = 256
HALO = 16
PAIR = 2
F32 = jnp.float32
BF16 = jnp.bfloat16
VMEM_LIMIT = 48 * 1024 * 1024
LIGHT = pl.CostEstimate(flops=1, bytes_accessed=1, transcendentals=0)


def swapped(value, axis, bit):
    size = lax.axis_size(axis)
    return lax.ppermute(value, axis, [(i, i ^ bit) for i in range(size)])


def shifted(value, axis, by):
    size = lax.axis_size(axis)
    return lax.ppermute(value, axis, [(i, i + by) for i in range(size - by)])


def cut(value, index, size, axis):
    return lax.dynamic_slice_in_dim(value, index * size, size, axis)


def after(value, *others):
    return lax.optimization_barrier((value, *others))[0]


ORDER = (
    (("x6", "z4", "x3", "x5"), ("x1", "x2", "x4", "z1")),
    (("t1", "z2", "w1", "w4"), ("x3", "x5", "x6", "t0")),
    (("x7", "w2", "z5"), ("z2", "w1", "z4")),
    (("t2", "z6", "z3", "w5"), ("t1", "x7", "w2", "z5", "w4")),
    (("w6",), ("w4", "w2")),
    (("z7",), ("z6", "z3", "w5", "t2")),
    (("w3",), ("z7",)),
)
WAITS = {send: waits for sends, waits in ORDER for send in sends}


class Sends:
    def __init__(self, own, given, quarter):
        self.own, self.given, self.quarter = own, given, quarter
        self.made = {}

    def get(self, kind, mask):
        name = f"{kind}{mask}"
        if name not in self.made:
            self.made[name] = self.tokens(mask) if kind == "t" else self.piece(kind, mask)
        return self.made[name]

    def waiting(self, kind, mask, value):
        others = [self.get(name[0], int(name[1:])) for name in WAITS.get(f"{kind}{mask}", ())]
        return after(value, *others) if others else value

    def piece(self, kind, mask):
        if mask == 0:
            return self.own[kind]
        if mask == PAIR:
            bit, value = PAIR, self.given[kind]
        else:
            bit = 1 if mask & 1 else 1 << (mask.bit_length() - 1)
            value = self.get(kind, mask ^ bit)
        return swapped(self.waiting(kind, mask, value), "seq", bit)

    def tokens(self, step):
        if step == 0:
            return swapped(self.waiting("t", 0, self.quarter), "seq", PAIR)
        if step == 1:
            value = self.get("t", 0)[None]
            bit = lax.axis_size("head") // 2
            while bit > 1:
                got = swapped(self.waiting("t", 1, value), "head", bit)
                value = jnp.concatenate([value, got])
                bit //= 2
            return value
        return swapped(self.waiting("t", 2, self.get("t", 1)), "head", 1)


def natural(value, axis_name, bit, axis):
    other = swapped(value, axis_name, bit)
    low = (lax.axis_index(axis_name) & bit) == 0
    return jnp.where(
        low, jnp.concatenate([value, other], axis=axis), jnp.concatenate([other, value], axis=axis)
    )


def by_xor(values, index):
    bit = 1
    while bit < len(values):
        flip = (index & bit) != 0
        values = [jnp.where(flip, values[j ^ bit], values[j]) for j in range(len(values))]
        bit *= 2
    return values


def dot(a, b):
    return jnp.dot(a, b, preferred_element_type=F32)


def front_kernel(
    first_ref, x_ref, bc_ref, tx_ref, tbc_ref, kx_ref, kbc_ref, dec_ref, xc_ref, bcc_ref, f_ref
):
    rows = xc_ref.shape[1]
    for r in range(2):
        is_first = first_ref[r] == 1

        def conv(pre_ref, tail_ref, k_ref):
            halo = jnp.where(is_first, tail_ref[...].astype(F32), pre_ref[r, :HALO].astype(F32))
            body = pre_ref[r, HALO:].astype(F32)
            whole = jnp.concatenate([halo, body], axis=0)
            taps = k_ref.shape[0]
            total = jnp.zeros(body.shape, F32)
            for k in range(taps):
                start = HALO - (taps - 1) + k
                total = total + k_ref[k : k + 1, :] * whole[start : start + rows]
            return (total * jax.nn.sigmoid(total)).astype(BF16)

        x_val = conv(x_ref, tx_ref, kx_ref)
        bc_val = conv(bc_ref, tbc_ref, kbc_ref)
        xc_ref[r] = x_val
        bcc_ref[r] = bc_val
        decayed = (x_val.astype(F32) * dec_ref[r]).astype(BF16)
        nstate = bc_val.shape[1] // 2
        for start in range(0, rows, Q):
            f_ref[r, start // Q] = lax.dot_general(
                bc_val[start : start + Q, :nstate],
                decayed[start : start + Q],
                (((0,), (0,)), ((), ())),
                preferred_element_type=F32,
            )


def intra_kernel(heads, x_ref, bc_ref, cum_ref, cumt_ref, y_ref):
    nstate = bc_ref.shape[2] // 2
    span = x_ref.shape[1]
    head_dim = x_ref.shape[2] // heads
    b_val = bc_ref[0, :, :nstate]
    c_val = bc_ref[0, :, nstate:]
    scores = lax.dot_general(c_val, b_val, (((1,), (1,)), ((), ())), preferred_element_type=F32)
    lower = lax.broadcasted_iota(jnp.int32, (span, span), 0) >= lax.broadcasted_iota(jnp.int32, (span, span), 1)
    scores = jnp.where(lower, scores, 0.0)
    pair = 128 // head_dim
    for start in range(0, heads, pair):
        outs = []
        for h in range(start, start + pair):
            diff = cum_ref[0, :, h : h + 1] - cumt_ref[0, 0, h : h + 1, :]
            weights = (jnp.exp(jnp.where(lower, diff, 0.0)) * scores).astype(BF16)
            outs.append(dot(weights, x_ref[0, :, h * head_dim : (h + 1) * head_dim]))
        y_ref[0, :, start * head_dim : (start + pair) * head_dim] = jnp.concatenate(outs, axis=1)


def gate_kernel(y_ref, x_ref, bc_ref, st_ref, e_ref, skip_ref, z_ref, gain_ref, g_ref, ss_ref):
    nstate = st_ref.shape[2]
    c_val = bc_ref[0, :, nstate:]
    state = st_ref[0, 0]
    high = state.astype(BF16)
    low = (state - high.astype(F32)).astype(BF16)
    carried = dot(c_val, high) + dot(c_val, low)
    y_val = (y_ref[0] + e_ref[0] * carried) / nstate + skip_ref[...] * x_ref[0].astype(F32)
    z_val = z_ref[0].astype(F32)
    gated = y_val * (z_val * jax.nn.sigmoid(z_val))
    g_ref[0] = (gated * gain_ref[...]).astype(BF16)
    total = jnp.sum(gated * gated, axis=1, keepdims=True)
    ss_ref[0] = jnp.broadcast_to(total, ss_ref.shape[1:])


def params(grid):
    return pltpu.CompilerParams(dimension_semantics=("arbitrary",) * grid, vmem_limit_bytes=VMEM_LIMIT)


def whole_block(shape):
    return pl.BlockSpec(shape, lambda *_: (0,) * len(shape))


def front(first, x_pre, bc_pre, tail_x, tail_bc, conv_x, conv_bc, decay):
    rows, chans = x_pre.shape[1] - HALO, x_pre.shape[2]
    bcw = bc_pre.shape[2]
    return pl.pallas_call(
        front_kernel,
        in_specs=[pl.BlockSpec(memory_space=pltpu.SMEM)] + [pl.BlockSpec(memory_space=pltpu.VMEM)] * 7,
        out_specs=[pl.BlockSpec(memory_space=pltpu.VMEM)] * 3,
        out_shape=[
            jax.ShapeDtypeStruct((2, rows, chans), BF16),
            jax.ShapeDtypeStruct((2, rows, bcw), BF16),
            jax.ShapeDtypeStruct((2, rows // Q, bcw // 2, chans), F32),
        ],
        compiler_params=pltpu.CompilerParams(vmem_limit_bytes=VMEM_LIMIT),
        cost_estimate=LIGHT,
        name="front",
    )(first, x_pre, bc_pre, tail_x, tail_bc, conv_x, conv_bc, decay)


def project_kernel(depth, with_halo, one_weight, place_ref, *refs):
    refs = list(refs)
    out_ref = refs.pop()
    halo_ref = refs.pop(0) if with_halo else None
    tokens_ref, others_ref = refs[:2]
    rows = tokens_ref.shape[0]
    lead = HALO if with_halo else 0
    totals = [None] * 3
    for k in range(place_ref.shape[1]):
        start = pl.multiple_of(place_ref[0, k], depth)
        place = pl.multiple_of(place_ref[2, k], depth)
        weight = refs[2][pl.ds(start, depth), :] if one_weight else refs[2 + k][:depth]
        lefts = [tokens_ref[:, pl.ds(start, depth)], others_ref[place_ref[1, k], :rows, pl.ds(place, depth)]]
        if with_halo:
            lefts.append(halo_ref[:, pl.ds(start, depth)])
        for i, left in enumerate(lefts):
            term = dot(left, weight)
            totals[i] = term if totals[i] is None else totals[i] + term
    for r in range(2):
        out_ref[r, lead:] = totals[r].astype(BF16)
        if with_halo:
            out_ref[r, :lead] = totals[2][r * HALO : (r + 1) * HALO].astype(BF16)


def project(places, depth, tokens, others, weights, halo=None):
    rows = tokens.shape[0] + (0 if halo is None else HALO)
    chans = weights[0].shape[1]
    operands = ([] if halo is None else [halo]) + [tokens, others] + list(weights)
    return pl.pallas_call(
        functools.partial(project_kernel, depth, halo is not None, len(weights) == 1),
        in_specs=[pl.BlockSpec(memory_space=pltpu.SMEM)]
        + [pl.BlockSpec(memory_space=pltpu.VMEM)] * len(operands),
        out_specs=pl.BlockSpec(memory_space=pltpu.VMEM),
        out_shape=jax.ShapeDtypeStruct((2, rows, chans), BF16),
        compiler_params=pltpu.CompilerParams(vmem_limit_bytes=VMEM_LIMIT),
        cost_estimate=LIGHT,
        name="project",
    )(places, *operands)


def intra(x_conv, bc_conv, cum, cumt, heads):
    _, rows, chans = x_conv.shape
    bcw = bc_conv.shape[2]
    blocks = rows // Q

    def tile(w):
        return pl.BlockSpec((1, Q, w), lambda r, i: (r, i, 0))

    return pl.pallas_call(
        functools.partial(intra_kernel, heads),
        grid=(2, blocks),
        in_specs=[tile(chans), tile(bcw), tile(heads), pl.BlockSpec((1, 1, heads, Q), lambda r, i: (r, i, 0, 0))],
        out_specs=tile(chans),
        out_shape=jax.ShapeDtypeStruct((2, rows, chans), F32),
        compiler_params=params(2),
        cost_estimate=LIGHT,
        name="intra",
    )(x_conv, bc_conv, cum, cumt)


def gate(y_in, x_conv, bc_conv, state, grown, skip, z_val, gain):
    _, rows, chans = x_conv.shape
    bcw = bc_conv.shape[2]

    def tile(w):
        return pl.BlockSpec((1, Q, w), lambda r, i: (r, i, 0))

    return pl.pallas_call(
        gate_kernel,
        grid=(2, rows // Q),
        in_specs=[
            tile(chans),
            tile(chans),
            tile(bcw),
            pl.BlockSpec((1, 1, bcw // 2, chans), lambda r, i: (r, i, 0, 0)),
            tile(chans),
            whole_block((1, chans)),
            tile(chans),
            whole_block((1, chans)),
        ],
        out_specs=[tile(chans), tile(128)],
        out_shape=[
            jax.ShapeDtypeStruct((2, rows, chans), BF16),
            jax.ShapeDtypeStruct((2, rows, 128), F32),
        ],
        compiler_params=params(2),
        cost_estimate=LIGHT,
        name="gate",
    )(y_in, x_conv, bc_conv, state, grown, skip, z_val, gain)


def local(
    tokens,
    w_xz,
    w_bc,
    conv_x,
    conv_bc,
    tail_x,
    tail_bc,
    decay_code,
    skip_gain,
    state_in,
    norm_gain,
    w_out,
):
    rows = tokens.shape[0]
    all_heads, head_dim, nstate = state_in.shape
    seq_count = lax.axis_size("seq")
    head_count = lax.axis_size("head")
    inner = all_heads * head_dim * head_count
    me = lax.axis_index("seq")
    mine = lax.axis_index("head")
    half = (me // PAIR) % 2
    heads = all_heads // 2
    chans = heads * head_dim
    depth = w_xz.shape[0]

    lag = conv_x.shape[0] - 1
    code_sums = jnp.sum(decay_code, axis=0)
    digits = jnp.stack([(code_sums >> (8 * j)) & 255 for j in range(4)]).reshape(1, -1).astype(BF16)
    last_rows = tokens[rows - lag :].reshape(-1, chans)
    halo_rows = last_rows.shape[0]
    spare = -(halo_rows + 1) % 16
    extra = jnp.concatenate(
        [last_rows, jnp.pad(digits, ((0, spare), (0, chans - digits.shape[1])))], axis=0
    )

    share = tokens.shape[1] // head_count
    codes = decay_code.T
    given = cut(codes, 1 - half, heads, 0)
    given = jnp.stack([(given >> (8 * j)) & 255 for j in range(3)]).reshape(-1, share).astype(BF16)
    code_rows = given.shape[0]
    given = jnp.pad(given, ((0, -code_rows % 16), (0, 0)))

    flat_w = lax.optimization_barrier(w_xz.reshape(depth, -1))
    full = flat_w.shape[1] // 2
    x_w, z_w = flat_w[:, :full], flat_w[:, full:]
    own = {
        "x": jnp.concatenate([cut(x_w, half, chans, 1), extra]),
        "z": cut(z_w, half, chans, 1),
        "w": cut(w_out, half, chans, 0),
    }
    other_half = {
        "x": jnp.concatenate([cut(x_w, 1 - half, chans, 1), extra]),
        "z": cut(z_w, 1 - half, chans, 1),
        "w": cut(w_out, 1 - half, chans, 0),
    }
    sends = Sends(own, other_half, jnp.concatenate([cut(tokens, mine, share, 1), given]))
    masks = list(range(seq_count))
    x_pieces, z_pieces, out_pieces = [{mask: sends.get(kind, mask) for mask in masks} for kind in "xzw"]

    others = jnp.concatenate([sends.get("t", 1), sends.get("t", 2)])
    ranges = [me, me ^ PAIR]
    extras = jnp.stack([x_pieces[mask][depth:] for mask in range(seq_count)])

    def rows_before(place):
        got = lax.dynamic_index_in_dim(extras, (me ^ (place - 1)) & (seq_count - 1), 0, keepdims=False)
        return jnp.pad(got[:halo_rows].reshape(lag, -1), ((HALO - lag, 0), (0, 0)))

    halo = jnp.concatenate([rows_before(place) for place in ranges], axis=0)

    starts = [(me ^ mask) * depth for mask in masks]
    blocks = [a // share ^ mine for a in starts]
    blocks = [(b >> 1) + (b & 1) * (head_count // 2) for b in blocks]
    spots = [starts, blocks, [a % share for a in starts]]
    spots = jnp.stack([jnp.stack([jnp.int32(a) for a in row]) for row in spots])

    part = depth // head_count
    w_bc_all = lax.all_gather(cut(w_bc, mine, part, 0), ("seq", "head"), axis=0, tiled=True)
    bc_pre = project(spots, depth, tokens, others, [w_bc_all], halo)
    x_pre = project(spots, depth, tokens, others, list(x_pieces.values()), halo)
    z_val = project(spots, depth, tokens, others, list(z_pieces.values()))

    per_code = -1.0 / (16.0 * rows * seq_count)
    got = sends.get("t", 0)[rows : rows + code_rows].astype(F32).reshape(3, heads, rows)
    other_codes = got[0] + 256.0 * got[1] + 65536.0 * got[2]
    ld = jnp.stack([cut(codes, half, heads, 0).astype(F32), other_codes]) * per_code
    blocks = rows // Q
    cumt = jnp.cumsum(ld.reshape(2, heads, blocks, Q), axis=3).transpose(0, 2, 1, 3)
    cum = cumt.transpose(0, 1, 3, 2)
    ends = cum[:, :, -1:, :]
    remaining = jnp.repeat(jnp.exp(ends - cum).reshape(2, rows, heads), head_dim, axis=2)
    block_decay = jnp.repeat(jnp.exp(ends), head_dim, axis=3)
    cum = cum.reshape(2, rows, heads)
    grown = jnp.repeat(jnp.exp(cum), head_dim, axis=2)
    totals = jnp.stack([x_pieces[mask][depth + halo_rows] for mask in masks])
    totals = totals[:, : 4 * all_heads].astype(F32).reshape(-1, 4, all_heads)
    totals = sum(totals[:, j] * 256.0**j for j in range(4)) * per_code
    totals = cut(totals, half, heads, 1)
    places = me ^ jnp.array(masks, jnp.int32)

    def decay_between(low, high):
        chosen = jnp.where((places >= low) & (places < high), 1.0, 0.0)[:, None]
        return jnp.repeat(jnp.exp(jnp.sum(chosen * totals, axis=0)), head_dim)[None, :]

    first = jnp.stack([(r == 0).astype(jnp.int32) for r in ranges])

    def padded(tail):
        return jnp.pad(tail, ((HALO - tail.shape[0], 0), (0, 0)))

    x_conv, bc_conv, added = front(
        after(first, sends.get("w", PAIR)),
        x_pre,
        bc_pre,
        padded(cut(tail_x, half, chans, 1)),
        padded(tail_bc),
        cut(conv_x, half, chans, 1),
        conv_bc,
        remaining,
    )

    inside = [jnp.zeros_like(added[:, 0])]
    for b in range(blocks):
        inside.append(block_decay[:, b] * inside[-1] + added[:, b])
    ending = inside.pop()

    group = 4
    across = swapped(ending.astype(BF16), "seq", 1).astype(F32)
    ended = {0: ending[0], PAIR: ending[1], 1: across[0], PAIR | 1: across[1]}
    base = (me // group) * group
    groups = seq_count // group
    total = 0.0
    for mask, value in ended.items():
        total = total + decay_between((me ^ mask) + 1, base + group) * value
    carry = shifted(total.astype(BF16), "seq", group).astype(F32)
    covered = 1
    while covered < groups - 1:
        more = shifted(carry.astype(BF16), "seq", group * covered).astype(F32)
        carry = carry + decay_between(base - group * covered, base) * more
        covered *= 2
    begin = cut(state_in, half, heads, 0).transpose(2, 0, 1).reshape(nstate, chans)
    incoming = []
    for place in ranges:
        value = decay_between(0, place) * begin + decay_between(base, place) * carry
        for mask, ended_value in ended.items():
            scale = jnp.where((me ^ mask) < place, decay_between((me ^ mask) + 1, place), 0.0)
            value = value + scale * ended_value
        incoming.append(value)
    opening = jnp.stack(incoming)
    states = []
    for b in range(blocks):
        states.append(opening + inside[b])
        opening = block_decay[:, b] * opening

    y_in = intra(x_conv, bc_conv, cum, cumt, heads)
    gated, squares = gate(
        y_in,
        x_conv,
        bc_conv,
        jnp.stack(states, axis=1),
        grown,
        jnp.repeat(cut(skip_gain, half, heads, 0), head_dim)[None, :],
        z_val,
        after(cut(norm_gain, half, chans, 0)[None, :], out_pieces[PAIR | 1]),
    )

    per = seq_count // head_count
    relation = (me // per) ^ mine
    flat = gated.reshape(2 * rows, chans)

    def by_destination(low):
        return by_xor([out_pieces[q * per + low] for q in range(head_count)], relation)

    def send_far(weights):
        far = jnp.concatenate(weights[1::2], axis=1)
        return swapped(dot(flat, far).astype(BF16), "head", 1).astype(F32)

    def fold_head(parts):
        bit = 2
        while len(parts) > 1:
            sent = jnp.concatenate(parts[1::2], axis=1) if len(parts) > 2 else parts[1]
            got = swapped(sent.astype(BF16), "head", bit).astype(F32)
            parts = columns_added(parts[::2], got)
            bit *= 2
        return parts[0]

    def columns_added(parts, got):
        width = parts[0].shape[1]
        return [part + got[:, i * width : (i + 1) * width] for i, part in enumerate(parts)]

    def swap_pair(value):
        return swapped(value.astype(BF16), "seq", PAIR).astype(F32)

    squares = squares[0, :, 0] + swapped(squares[1, :, 0], "seq", PAIR)
    paired = squares
    bit = head_count // 2
    while bit >= 1:
        upper = squares
        squares = squares + swapped(squares, "head", bit)
        bit //= 2
    scale = lax.rsqrt(squares / inner + 1e-05)[:, None]

    done = {}
    for low in range(0, per, 2):
        weights = by_destination(low)
        got_far = send_far(weights)
        parts = columns_added([dot(flat, w) for w in weights[::2]], got_far)
        parts = [after(part, upper) if i else part for i, part in enumerate(parts)]
        whole = fold_head(parts)
        done[low] = whole[:rows] + swap_pair(whole[rows:])
    flat = after(flat, paired)
    for low in range(1, per, 2):
        weights = by_destination(low)
        got_far = send_far(weights)
        near = weights[::2]
        away = swap_pair(dot(gated[1], jnp.concatenate(near, axis=1)) + got_far[rows:])
        here = columns_added([dot(gated[0], w) for w in near], got_far[:rows])
        done[low] = fold_head(columns_added(here, away))

    result = by_xor([done[low] for low in range(per)], me % per)
    return jnp.concatenate([(piece * scale).astype(BF16) for piece in result], axis=1)


def solution(mesh):
    return jax.shard_map(
        local,
        mesh=mesh,
        in_specs=(
            P("seq", None),
            P("seq", None, "head"),
            P("seq", None),
            P(None, "head"),
            P(),
            P(None, "head"),
            P(),
            P("seq", "head"),
            P("head"),
            P("head", None, None),
            P("head"),
            P("head", "seq"),
        ),
        out_specs=P("seq", "head"),
        check_vma=False,
    )
```

```python
import functools

import jax
import jax.numpy as jnp
from jax import lax
from jax.experimental import pallas as pl
from jax.experimental.pallas import tpu as pltpu
from jax.sharding import PartitionSpec as P

Q = 256
HALO = 16
PAIR = 2
F32 = jnp.float32
BF16 = jnp.bfloat16
VMEM_LIMIT = 48 * 1024 * 1024
LIGHT = pl.CostEstimate(flops=1, bytes_accessed=1, transcendentals=0)


def swapped(value, axis, bit):
    size = lax.axis_size(axis)
    return lax.ppermute(value, axis, [(i, i ^ bit) for i in range(size)])


def shifted(value, axis, by):
    size = lax.axis_size(axis)
    return lax.ppermute(value, axis, [(i, i + by) for i in range(size - by)])


def cut(value, index, size, axis):
    return lax.dynamic_slice_in_dim(value, index * size, size, axis)


def after(value, *others):
    return lax.optimization_barrier((value, *others))[0]


ORDER = (
    (("x6", "z4", "x3", "x5"), ("x1", "x2", "x4", "z1")),
    (("t1", "z2", "w1", "w4"), ("x3", "x5", "x6", "t0")),
    (("x7", "w2", "z5"), ("z2", "w1", "z4")),
    (("t2", "z6", "z3", "w5"), ("t1", "x7", "w2", "z5", "w4")),
    (("w6",), ("w4", "w2")),
    (("z7",), ("z6", "z3", "w5", "t2")),
    (("w3",), ("z7",)),
)
WAITS = {send: waits for sends, waits in ORDER for send in sends}


class Sends:
    def __init__(self, own, given, quarter):
        self.own, self.given, self.quarter = own, given, quarter
        self.made = {}

    def get(self, kind, mask):
        name = f"{kind}{mask}"
        if name not in self.made:
            self.made[name] = self.tokens(mask) if kind == "t" else self.piece(kind, mask)
        return self.made[name]

    def waiting(self, kind, mask, value):
        others = [self.get(name[0], int(name[1:])) for name in WAITS.get(f"{kind}{mask}", ())]
        return after(value, *others) if others else value

    def piece(self, kind, mask):
        if mask == 0:
            return self.own[kind]
        if mask == PAIR:
            bit, value = PAIR, self.given[kind]
        else:
            bit = 1 if mask & 1 else 1 << (mask.bit_length() - 1)
            value = self.get(kind, mask ^ bit)
        return swapped(self.waiting(kind, mask, value), "seq", bit)

    def tokens(self, step):
        if step == 0:
            return swapped(self.waiting("t", 0, self.quarter), "seq", PAIR)
        if step == 1:
            value = self.get("t", 0)[None]
            bit = lax.axis_size("head") // 2
            while bit > 1:
                got = swapped(self.waiting("t", 1, value), "head", bit)
                value = jnp.concatenate([value, got])
                bit //= 2
            return value
        return swapped(self.waiting("t", 2, self.get("t", 1)), "head", 1)


def natural(value, axis_name, bit, axis):
    other = swapped(value, axis_name, bit)
    low = (lax.axis_index(axis_name) & bit) == 0
    return jnp.where(
        low, jnp.concatenate([value, other], axis=axis), jnp.concatenate([other, value], axis=axis)
    )


def by_xor(values, index):
    bit = 1
    while bit < len(values):
        flip = (index & bit) != 0
        values = [jnp.where(flip, values[j ^ bit], values[j]) for j in range(len(values))]
        bit *= 2
    return values


def dot(a, b):
    return jnp.dot(a, b, preferred_element_type=F32)


def front_kernel(
    first_ref, x_ref, bc_ref, tx_ref, tbc_ref, kx_ref, kbc_ref, dec_ref, xc_ref, bcc_ref, f_ref
):
    rows = xc_ref.shape[1]
    for r in range(2):
        is_first = first_ref[r] == 1

        def conv(pre_ref, tail_ref, k_ref):
            halo = jnp.where(is_first, tail_ref[...].astype(F32), pre_ref[r, :HALO].astype(F32))
            body = pre_ref[r, HALO:].astype(F32)
            whole = jnp.concatenate([halo, body], axis=0)
            taps = k_ref.shape[0]
            total = jnp.zeros(body.shape, F32)
            for k in range(taps):
                start = HALO - (taps - 1) + k
                total = total + k_ref[k : k + 1, :] * whole[start : start + rows]
            return (total * jax.nn.sigmoid(total)).astype(BF16)

        x_val = conv(x_ref, tx_ref, kx_ref)
        bc_val = conv(bc_ref, tbc_ref, kbc_ref)
        xc_ref[r] = x_val
        bcc_ref[r] = bc_val
        decayed = (x_val.astype(F32) * dec_ref[r]).astype(BF16)
        nstate = bc_val.shape[1] // 2
        for start in range(0, rows, Q):
            f_ref[r, start // Q] = lax.dot_general(
                bc_val[start : start + Q, :nstate],
                decayed[start : start + Q],
                (((0,), (0,)), ((), ())),
                preferred_element_type=F32,
            )


def intra_kernel(heads, x_ref, bc_ref, cum_ref, cumt_ref, y_ref):
    nstate = bc_ref.shape[2] // 2
    span = x_ref.shape[1]
    head_dim = x_ref.shape[2] // heads
    b_val = bc_ref[0, :, :nstate]
    c_val = bc_ref[0, :, nstate:]
    scores = lax.dot_general(c_val, b_val, (((1,), (1,)), ((), ())), preferred_element_type=F32)
    lower = lax.broadcasted_iota(jnp.int32, (span, span), 0) >= lax.broadcasted_iota(jnp.int32, (span, span), 1)
    scores = jnp.where(lower, scores, 0.0)
    pair = 128 // head_dim
    for start in range(0, heads, pair):
        outs = []
        for h in range(start, start + pair):
            diff = cum_ref[0, :, h : h + 1] - cumt_ref[0, 0, h : h + 1, :]
            weights = (jnp.exp(jnp.where(lower, diff, 0.0)) * scores).astype(BF16)
            outs.append(dot(weights, x_ref[0, :, h * head_dim : (h + 1) * head_dim]))
        y_ref[0, :, start * head_dim : (start + pair) * head_dim] = jnp.concatenate(outs, axis=1)


def gate_kernel(y_ref, x_ref, bc_ref, st_ref, e_ref, skip_ref, z_ref, gain_ref, g_ref, ss_ref):
    nstate = st_ref.shape[2]
    c_val = bc_ref[0, :, nstate:]
    state = st_ref[0, 0]
    high = state.astype(BF16)
    low = (state - high.astype(F32)).astype(BF16)
    carried = dot(c_val, high) + dot(c_val, low)
    y_val = (y_ref[0] + e_ref[0] * carried) / nstate + skip_ref[...] * x_ref[0].astype(F32)
    z_val = z_ref[0].astype(F32)
    gated = y_val * (z_val * jax.nn.sigmoid(z_val))
    g_ref[0] = (gated * gain_ref[...]).astype(BF16)
    total = jnp.sum(gated * gated, axis=1, keepdims=True)
    ss_ref[0] = jnp.broadcast_to(total, ss_ref.shape[1:])


def finish_kernel(place_ref, scale_ref, *refs):
    out_ref = refs[-1]
    count = (len(refs) - 1) // 2
    width = refs[0].shape[1]
    for i in range(count):
        value = (refs[i][...] + refs[count + i][...].astype(F32)) * scale_ref[:, :1]
        start = pl.multiple_of(place_ref[i] * width, width)
        out_ref[:, pl.ds(start, width)] = value.astype(BF16)


def finish(places, scale, kept, received):
    rows, width = received[0].shape
    tile = min(rows, 256)

    def part(value):
        return pl.BlockSpec((tile, value.shape[1]), lambda i: (i, 0))

    return pl.pallas_call(
        finish_kernel,
        grid=(rows // tile,),
        in_specs=[pl.BlockSpec(memory_space=pltpu.SMEM)] + [part(v) for v in (scale, *kept, *received)],
        out_specs=pl.BlockSpec((tile, width * len(kept)), lambda i: (i, 0)),
        out_shape=jax.ShapeDtypeStruct((rows, width * len(kept)), BF16),
        compiler_params=params(1),
        cost_estimate=LIGHT,
        name="finish",
    )(places, scale, *kept, *received)


def params(grid):
    return pltpu.CompilerParams(dimension_semantics=("arbitrary",) * grid, vmem_limit_bytes=VMEM_LIMIT)


def whole_block(shape):
    return pl.BlockSpec(shape, lambda *_: (0,) * len(shape))


def front(first, x_pre, bc_pre, tail_x, tail_bc, conv_x, conv_bc, decay):
    rows, chans = x_pre.shape[1] - HALO, x_pre.shape[2]
    bcw = bc_pre.shape[2]
    return pl.pallas_call(
        front_kernel,
        in_specs=[pl.BlockSpec(memory_space=pltpu.SMEM)] + [pl.BlockSpec(memory_space=pltpu.VMEM)] * 7,
        out_specs=[pl.BlockSpec(memory_space=pltpu.VMEM)] * 3,
        out_shape=[
            jax.ShapeDtypeStruct((2, rows, chans), BF16),
            jax.ShapeDtypeStruct((2, rows, bcw), BF16),
            jax.ShapeDtypeStruct((2, rows // Q, bcw // 2, chans), F32),
        ],
        compiler_params=pltpu.CompilerParams(vmem_limit_bytes=VMEM_LIMIT),
        cost_estimate=LIGHT,
        name="front",
    )(first, x_pre, bc_pre, tail_x, tail_bc, conv_x, conv_bc, decay)


def project_kernel(depth, with_halo, one_weight, place_ref, *refs):
    refs = list(refs)
    out_ref = refs.pop()
    halo_ref = refs.pop(0) if with_halo else None
    tokens_ref, others_ref = refs[:2]
    rows = tokens_ref.shape[0]
    lead = HALO if with_halo else 0
    totals = [None] * 3
    for k in range(place_ref.shape[1]):
        start = pl.multiple_of(place_ref[0, k], depth)
        place = pl.multiple_of(place_ref[2, k], depth)
        weight = refs[2][pl.ds(start, depth), :] if one_weight else refs[2 + k][:depth]
        lefts = [tokens_ref[:, pl.ds(start, depth)], others_ref[place_ref[1, k], :rows, pl.ds(place, depth)]]
        if with_halo:
            lefts.append(halo_ref[:, pl.ds(start, depth)])
        for i, left in enumerate(lefts):
            term = dot(left, weight)
            totals[i] = term if totals[i] is None else totals[i] + term
    for r in range(2):
        out_ref[r, lead:] = totals[r].astype(BF16)
        if with_halo:
            out_ref[r, :lead] = totals[2][r * HALO : (r + 1) * HALO].astype(BF16)


def project(places, depth, tokens, others, weights, halo=None):
    rows = tokens.shape[0] + (0 if halo is None else HALO)
    chans = weights[0].shape[1]
    operands = ([] if halo is None else [halo]) + [tokens, others] + list(weights)
    return pl.pallas_call(
        functools.partial(project_kernel, depth, halo is not None, len(weights) == 1),
        in_specs=[pl.BlockSpec(memory_space=pltpu.SMEM)]
        + [pl.BlockSpec(memory_space=pltpu.VMEM)] * len(operands),
        out_specs=pl.BlockSpec(memory_space=pltpu.VMEM),
        out_shape=jax.ShapeDtypeStruct((2, rows, chans), BF16),
        compiler_params=pltpu.CompilerParams(vmem_limit_bytes=VMEM_LIMIT),
        cost_estimate=LIGHT,
        name="project",
    )(places, *operands)


def intra(x_conv, bc_conv, cum, cumt, heads):
    _, rows, chans = x_conv.shape
    bcw = bc_conv.shape[2]
    blocks = rows // Q

    def tile(w):
        return pl.BlockSpec((1, Q, w), lambda r, i: (r, i, 0))

    return pl.pallas_call(
        functools.partial(intra_kernel, heads),
        grid=(2, blocks),
        in_specs=[tile(chans), tile(bcw), tile(heads), pl.BlockSpec((1, 1, heads, Q), lambda r, i: (r, i, 0, 0))],
        out_specs=tile(chans),
        out_shape=jax.ShapeDtypeStruct((2, rows, chans), F32),
        compiler_params=params(2),
        cost_estimate=LIGHT,
        name="intra",
    )(x_conv, bc_conv, cum, cumt)


def gate(y_in, x_conv, bc_conv, state, grown, skip, z_val, gain):
    _, rows, chans = x_conv.shape
    bcw = bc_conv.shape[2]

    def tile(w):
        return pl.BlockSpec((1, Q, w), lambda r, i: (r, i, 0))

    return pl.pallas_call(
        gate_kernel,
        grid=(2, rows // Q),
        in_specs=[
            tile(chans),
            tile(chans),
            tile(bcw),
            pl.BlockSpec((1, 1, bcw // 2, chans), lambda r, i: (r, i, 0, 0)),
            tile(chans),
            whole_block((1, chans)),
            tile(chans),
            whole_block((1, chans)),
        ],
        out_specs=[tile(chans), tile(128)],
        out_shape=[
            jax.ShapeDtypeStruct((2, rows, chans), BF16),
            jax.ShapeDtypeStruct((2, rows, 128), F32),
        ],
        compiler_params=params(2),
        cost_estimate=LIGHT,
        name="gate",
    )(y_in, x_conv, bc_conv, state, grown, skip, z_val, gain)


def local(
    tokens,
    w_xz,
    w_bc,
    conv_x,
    conv_bc,
    tail_x,
    tail_bc,
    decay_code,
    skip_gain,
    state_in,
    norm_gain,
    w_out,
):
    rows = tokens.shape[0]
    all_heads, head_dim, nstate = state_in.shape
    seq_count = lax.axis_size("seq")
    head_count = lax.axis_size("head")
    inner = all_heads * head_dim * head_count
    me = lax.axis_index("seq")
    mine = lax.axis_index("head")
    half = (me // PAIR) % 2
    heads = all_heads // 2
    chans = heads * head_dim
    depth = w_xz.shape[0]

    lag = conv_x.shape[0] - 1
    code_sums = jnp.sum(decay_code, axis=0)
    digits = jnp.stack([(code_sums >> (8 * j)) & 255 for j in range(4)]).reshape(1, -1).astype(BF16)
    last_rows = tokens[rows - lag :].reshape(-1, chans)
    halo_rows = last_rows.shape[0]
    spare = -(halo_rows + 1) % 16
    extra = jnp.concatenate(
        [last_rows, jnp.pad(digits, ((0, spare), (0, chans - digits.shape[1])))], axis=0
    )

    share = tokens.shape[1] // head_count
    codes = decay_code.T
    given = cut(codes, 1 - half, heads, 0)
    given = jnp.stack([(given >> (8 * j)) & 255 for j in range(3)]).reshape(-1, share).astype(BF16)
    code_rows = given.shape[0]
    given = jnp.pad(given, ((0, -code_rows % 16), (0, 0)))

    flat_w = lax.optimization_barrier(w_xz.reshape(depth, -1))
    full = flat_w.shape[1] // 2
    x_w, z_w = flat_w[:, :full], flat_w[:, full:]
    own = {
        "x": jnp.concatenate([cut(x_w, half, chans, 1), extra]),
        "z": cut(z_w, half, chans, 1),
        "w": cut(w_out, half, chans, 0),
    }
    other_half = {
        "x": jnp.concatenate([cut(x_w, 1 - half, chans, 1), extra]),
        "z": cut(z_w, 1 - half, chans, 1),
        "w": cut(w_out, 1 - half, chans, 0),
    }
    sends = Sends(own, other_half, jnp.concatenate([cut(tokens, mine, share, 1), given]))
    masks = list(range(seq_count))
    x_pieces, z_pieces, out_pieces = [{mask: sends.get(kind, mask) for mask in masks} for kind in "xzw"]

    others = jnp.concatenate([sends.get("t", 1), sends.get("t", 2)])
    ranges = [me, me ^ PAIR]
    extras = jnp.stack([x_pieces[mask][depth:] for mask in range(seq_count)])

    def rows_before(place):
        got = lax.dynamic_index_in_dim(extras, (me ^ (place - 1)) & (seq_count - 1), 0, keepdims=False)
        return jnp.pad(got[:halo_rows].reshape(lag, -1), ((HALO - lag, 0), (0, 0)))

    halo = jnp.concatenate([rows_before(place) for place in ranges], axis=0)

    starts = [(me ^ mask) * depth for mask in masks]
    blocks = [a // share ^ mine for a in starts]
    blocks = [(b >> 1) + (b & 1) * (head_count // 2) for b in blocks]
    spots = [starts, blocks, [a % share for a in starts]]
    spots = jnp.stack([jnp.stack([jnp.int32(a) for a in row]) for row in spots])

    part = depth // head_count
    w_bc_all = lax.all_gather(cut(w_bc, mine, part, 0), ("seq", "head"), axis=0, tiled=True)
    bc_pre = project(spots, depth, tokens, others, [w_bc_all], halo)
    x_pre = project(spots, depth, tokens, others, list(x_pieces.values()), halo)
    z_val = project(spots, depth, tokens, others, list(z_pieces.values()))

    per_code = -1.0 / (16.0 * rows * seq_count)
    got = sends.get("t", 0)[rows : rows + code_rows].astype(F32).reshape(3, heads, rows)
    other_codes = got[0] + 256.0 * got[1] + 65536.0 * got[2]
    ld = jnp.stack([cut(codes, half, heads, 0).astype(F32), other_codes]) * per_code
    blocks = rows // Q
    cumt = jnp.cumsum(ld.reshape(2, heads, blocks, Q), axis=3).transpose(0, 2, 1, 3)
    cum = cumt.transpose(0, 1, 3, 2)
    ends = cum[:, :, -1:, :]
    remaining = jnp.repeat(jnp.exp(ends - cum).reshape(2, rows, heads), head_dim, axis=2)
    block_decay = jnp.repeat(jnp.exp(ends), head_dim, axis=3)
    cum = cum.reshape(2, rows, heads)
    grown = jnp.repeat(jnp.exp(cum), head_dim, axis=2)
    totals = jnp.stack([x_pieces[mask][depth + halo_rows] for mask in masks])
    totals = totals[:, : 4 * all_heads].astype(F32).reshape(-1, 4, all_heads)
    totals = sum(totals[:, j] * 256.0**j for j in range(4)) * per_code
    totals = cut(totals, half, heads, 1)
    places = me ^ jnp.array(masks, jnp.int32)

    def decay_between(low, high):
        chosen = jnp.where((places >= low) & (places < high), 1.0, 0.0)[:, None]
        return jnp.repeat(jnp.exp(jnp.sum(chosen * totals, axis=0)), head_dim)[None, :]

    first = jnp.stack([(r == 0).astype(jnp.int32) for r in ranges])

    def padded(tail):
        return jnp.pad(tail, ((HALO - tail.shape[0], 0), (0, 0)))

    x_conv, bc_conv, added = front(
        after(first, sends.get("w", PAIR)),
        x_pre,
        bc_pre,
        padded(cut(tail_x, half, chans, 1)),
        padded(tail_bc),
        cut(conv_x, half, chans, 1),
        conv_bc,
        remaining,
    )

    inside = [jnp.zeros_like(added[:, 0])]
    for b in range(blocks):
        inside.append(block_decay[:, b] * inside[-1] + added[:, b])
    ending = inside.pop()

    group = 4
    across = swapped(ending.astype(BF16), "seq", 1).astype(F32)
    ended = {0: ending[0], PAIR: ending[1], 1: across[0], PAIR | 1: across[1]}
    base = (me // group) * group
    groups = seq_count // group
    total = 0.0
    for mask, value in ended.items():
        total = total + decay_between((me ^ mask) + 1, base + group) * value
    carry = shifted(total.astype(BF16), "seq", group).astype(F32)
    covered = 1
    while covered < groups - 1:
        more = shifted(carry.astype(BF16), "seq", group * covered).astype(F32)
        carry = carry + decay_between(base - group * covered, base) * more
        covered *= 2
    begin = cut(state_in, half, heads, 0).transpose(2, 0, 1).reshape(nstate, chans)
    incoming = []
    for place in ranges:
        value = decay_between(0, place) * begin + decay_between(base, place) * carry
        for mask, ended_value in ended.items():
            scale = jnp.where((me ^ mask) < place, decay_between((me ^ mask) + 1, place), 0.0)
            value = value + scale * ended_value
        incoming.append(value)
    opening = jnp.stack(incoming)
    states = []
    for b in range(blocks):
        states.append(opening + inside[b])
        opening = block_decay[:, b] * opening

    y_in = intra(x_conv, bc_conv, cum, cumt, heads)
    gated, squares = gate(
        y_in,
        x_conv,
        bc_conv,
        jnp.stack(states, axis=1),
        grown,
        jnp.repeat(cut(skip_gain, half, heads, 0), head_dim)[None, :],
        z_val,
        after(cut(norm_gain, half, chans, 0)[None, :], out_pieces[PAIR | 1]),
    )

    per = seq_count // head_count
    relation = (me // per) ^ mine
    flat = gated.reshape(2 * rows, chans)

    def by_destination(low):
        return by_xor([out_pieces[q * per + low] for q in range(head_count)], relation)

    def send_far(weights):
        far = jnp.concatenate(weights[1::2], axis=1)
        return swapped(dot(flat, far).astype(BF16), "head", 1).astype(F32)

    def fold_head(parts):
        bit = 2
        while len(parts) > 1:
            sent = jnp.concatenate(parts[1::2], axis=1) if len(parts) > 2 else parts[1]
            got = swapped(sent.astype(BF16), "head", bit)
            if len(parts) == 2:
                return parts[0], got
            parts = columns_added(parts[::2], got.astype(F32))
            bit *= 2

    def columns_added(parts, got):
        width = parts[0].shape[1]
        return [part + got[:, i * width : (i + 1) * width] for i, part in enumerate(parts)]

    def swap_pair(value):
        return swapped(value.astype(BF16), "seq", PAIR)

    squares = squares[0, :, 0] + swapped(squares[1, :, 0], "seq", PAIR)
    paired = squares
    bit = head_count // 2
    while bit >= 1:
        upper = squares
        squares = squares + swapped(squares, "head", bit)
        bit //= 2
    scale = lax.rsqrt(squares / inner + 1e-05)[:, None]

    done = {}
    for low in range(0, per, 2):
        weights = by_destination(low)
        got_far = send_far(weights)
        parts = columns_added([dot(flat, w) for w in weights[::2]], got_far)
        parts = [after(part, upper) if i else part for i, part in enumerate(parts)]
        whole, got = fold_head(parts)
        done[low] = whole, swap_pair(whole[rows:] + got[rows:].astype(F32)), got
    flat = after(flat, paired)
    for low in range(1, per, 2):
        weights = by_destination(low)
        got_far = send_far(weights)
        near = weights[::2]
        away = swap_pair(dot(gated[1], jnp.concatenate(near, axis=1)) + got_far[rows:])
        here = columns_added([dot(gated[0], w) for w in near], got_far[:rows])
        done[low] = fold_head(columns_added(here, away.astype(F32)))

    kept = [done[low][0][:rows] + done[low][2][:rows].astype(F32) if len(done[low]) == 3 else done[low][0] for low in range(per)]
    places = jnp.stack([jnp.int32(low ^ (me % per)) for low in range(per)])
    scale = jnp.broadcast_to(scale, (rows, 128))
    return finish(places, scale, kept, [done[low][1] for low in range(per)])


def solution(mesh):
    return jax.shard_map(
        local,
        mesh=mesh,
        in_specs=(
            P("seq", None),
            P("seq", None, "head"),
            P("seq", None),
            P(None, "head"),
            P(),
            P(None, "head"),
            P(),
            P("seq", "head"),
            P("head"),
            P("head", None, None),
            P("head"),
            P("head", "seq"),
        ),
        out_specs=P("seq", "head"),
        check_vma=False,
    )
```
